32 devices in a mesh: member: 2 (over y), band: 4 (over x, core), lev: 4 (over z).
Axes of the slice: x: 2, y: 2, z: 4, core: 2. Of those that a mesh axis runs over, the one named last changes fastest.
Arguments:
- spec_in: bfloat16 [4, 2, 4, 640, 1281], P('member', None, 'lev', 'band'), parts along dimension 0, may hold values from -0.0048828125 to 0.0048828125
- observation_weight: bfloat16 [32, 8, 5136], P(('band', 'lev'), 'member'), parts along dimension 1, may hold values from 0.099609375 to 1
- latitude_row_length: int32 [16], replicated, may hold values from 4116 to 5136, as said below
- wave_map: int32 [640], replicated, may hold values from 0 to 639, each once
- row_map: int32 [16], replicated, may hold values from 0 to 15, as said below
Outputs:
- grid_incr: float32 [32, 2, 8, 5136], P(('band', 'lev'), None, 'member'), parts along dimension 2
- spec_grad: bfloat16 [4, 2, 4, 640, 1281], P('member', None, 'lev', 'band'), parts along dimension 0
The draws below stay inside these ranges and needn't reach their ends.
There are 2 independent parts, one for each index of `member`. The reference program is written for one: setup_inputs(seed, part) draws one part's arguments, and reference() takes and returns one part's arrays. A program takes and returns all parts, laid end to end along the dimension named above; an argument that names none is the same for every part. Nothing has to cross between parts.
Inputs may be any that keep to these rules, and one draw needn't show every extreme that they name: `latitude_row_length`: row j has 4 i + 16 points for an octahedral row number i with 1025 <= i <= 1280; row 0 always has i = 1280. `wave_map`: each pair number appears once. row_map[j] is a device number band index * 4 + lev index. A quarter of the devices hold 2 rows, half hold 1 row, and a quarter hold none.
All inputs are finite; a program needn't handle non-finite values.
Results may differ from the reference program's by a relative error of at most 0.009.
Values may be sent and summed in bfloat16 or wider, within the bound.
A program may use at most 128 MiB of HBM per device.

```python
import math
import jax
import jax.numpy as jnp
from jax import lax

TRUNC = 1279
NHALF = 1280
ROW_DEV = 1
SUBW = 128
WAVES = 1280
PAIRS = 640
NCOL = 1281
LONGEST_ROW = 5136
MODEL_LEVELS = 4
OWNERS = 16
NLAT = 16
DEVICE_ROW_SLOTS = 2
TOTAL_SLOTS = 32
N_BAND = 4
N_LEV = 4


def draw_latitude_row_length(key, part):
    key = jax.random.fold_in(key, 11)
    lowest = NHALF - NHALF // 5 + 1
    cycles = jax.random.randint(key, (NLAT,), lowest, NHALF + 1, dtype=jnp.int32)
    cycles = cycles.at[0].set(NHALF)
    return (4 * cycles + 16).astype(jnp.int32)


def draw_row_map(key, part):
    key = jax.random.fold_in(key, 23)
    first_key, second_key = jax.random.split(key)
    devices = OWNERS
    ranking = jnp.zeros((devices,), jnp.int32).at[jax.random.permutation(first_key, devices)].set(jnp.arange(devices, dtype=jnp.int32))
    load = jnp.where(ranking < devices // 4, DEVICE_ROW_SLOTS, jnp.where(ranking < 3 * devices // 4, ROW_DEV, 0))
    owner = jnp.repeat(jnp.arange(devices, dtype=jnp.int32), DEVICE_ROW_SLOTS)
    place = jnp.tile(jnp.arange(DEVICE_ROW_SLOTS, dtype=jnp.int32), devices)
    unused = jnp.where(place < load[owner], 0, 1).astype(jnp.int32)
    picked = owner[jnp.argsort(unused, stable=True)[:NLAT]]
    return picked[jax.random.permutation(second_key, NLAT)].astype(jnp.int32)


def level_of(stream_key, extent, shards, smallest, high):
    def one(dim, parts):
        heights = jax.random.uniform(jax.random.fold_in(jax.random.fold_in(stream_key, 6), dim), (parts,), jnp.float32, smallest / len(shards), high / len(shards))
        return jnp.repeat(jnp.exp(heights), extent[dim] // parts).reshape((-1,) + (1,) * (len(extent) - dim - 1))

    loudness = one(*shards[0])
    for cut in shards[1:]:
        loudness = loudness * one(*cut)
    return loudness


def scatter_about(own_key, dims, scale, reach, cuts=(), held_as=jnp.bfloat16):
    level = level_of(own_key, dims, cuts, -0.22, 0.18) if cuts else 1.0
    values = jax.random.normal(own_key, dims, jnp.float32) * scale * level
    return jnp.minimum(jnp.maximum(values, -reach), reach).astype(held_as)


def setup_inputs(seed: int = 0, part: int = 0) -> dict:
    streams_of = jax.random.split(jax.random.key(seed), 6)
    part_keys = jax.random.split(jax.random.fold_in(streams_of[5], part), 6)
    spec_in = scatter_about(part_keys[0], (2, 2, MODEL_LEVELS, PAIRS, NCOL), (1.0 / (TRUNC + 1)), 0.0048828125, ((2, 4), (3, 4)))
    observation_weight = jnp.clip(jnp.exp(math.log(1.0) - 2.306499 * jax.random.uniform(part_keys[1], (TOTAL_SLOTS, MODEL_LEVELS, LONGEST_ROW), jnp.float32) ** level_of(part_keys[1], (TOTAL_SLOTS, MODEL_LEVELS, LONGEST_ROW), ((0, 16),), -0.2, 0.2)), 0.099609375, 1.0).astype(jnp.bfloat16)
    latitude_row_length = draw_latitude_row_length(jax.random.fold_in(streams_of[5], 71), part)
    wave_map = jax.random.permutation(streams_of[3], PAIRS).astype(jnp.int32)
    row_map = draw_row_map(jax.random.fold_in(streams_of[5], 71), part)
    return dict(spec_in=spec_in, observation_weight=observation_weight, latitude_row_length=latitude_row_length, wave_map=wave_map, row_map=row_map)


def rounded(values):
    return lax.optimization_barrier(values.astype(jnp.bfloat16)).astype(jnp.float32)

def latitudes(latitude_row_length, halves):
    cycle_no = ((latitude_row_length - 16) // 4).astype(jnp.float32)
    colat = math.pi * (cycle_no - 0.25) / (2.0 * halves + 0.5)
    north = jnp.arange(latitude_row_length.shape[0], dtype=jnp.int32) < latitude_row_length.shape[0] // 2
    return (jnp.where(north, jnp.cos(colat), -jnp.cos(colat)), jnp.log(jnp.sin(colat)))

def side_mask(pair_ids, truncation):
    column = jnp.arange(truncation + 2, dtype=jnp.int32)[None, :]
    first_side = column < truncation + 1 - pair_ids.astype(jnp.int32)[:, None]
    return jnp.stack([first_side, jnp.logical_not(first_side)], axis=2)

def legendre(pair_ids, cos_lat, log_sin, truncation):
    columns = truncation + 2
    column = jnp.arange(columns, dtype=jnp.int32)[None, :]
    first_order = pair_ids.astype(jnp.int32)[:, None]
    boundary = truncation + 1 - first_order
    first_side = column < boundary
    order_m = jnp.where(first_side, first_order, truncation - first_order).astype(jnp.float32)
    degree = jnp.where(first_side, first_order + column, column - 1).astype(jnp.float32)
    restart_first = column == 0
    restart_second = column == boundary
    restart = restart_first | restart_second
    counter = jnp.arange(1, truncation + 1, dtype=jnp.int32)
    log_terms = jnp.log(1.0 - 0.5 / counter.astype(jnp.float32))

    def log_start(orders):
        partial_sum = lax.optimization_barrier(jnp.sum(jnp.where(counter[None, :] <= orders, log_terms[None, :], 0.0), axis=1, keepdims=True))
        return 0.5 * (jnp.log(orders.astype(jnp.float32) + 0.5) + partial_sum)
    first_m = first_order.astype(jnp.float32)
    second_m = (truncation - first_order).astype(jnp.float32)
    diag_first = jnp.exp(log_start(first_order) + first_m * log_sin[None, :])
    diag_second = jnp.exp(log_start(truncation - first_order) + second_m * log_sin[None, :])

    def epsilon(values):
        upper = jnp.maximum(values * values - order_m * order_m, 0.0)
        lower = jnp.maximum(4.0 * values * values - 1.0, 1.0)
        return jnp.sqrt(upper / lower)
    divisor = jnp.where(restart, 1.0, epsilon(degree))
    slope = jnp.where(restart, 0.0, 1.0 / divisor)
    lagged = jnp.where(restart, 0.0, -epsilon(degree - 1.0) / divisor)

    def advance(carry, packed):
        older, oldest = carry
        slope_c, lagged_c, first_c, second_c = packed
        recurred = slope_c[:, None] * cos_lat[None, :] * older + lagged_c[:, None] * oldest
        value = jnp.where(first_c[:, None], diag_first, jnp.where(second_c[:, None], diag_second, recurred))
        fresh = first_c[:, None] | second_c[:, None]
        oldest = jnp.where(fresh, 0.0, older)
        return ((value, oldest), value)
    empty = jnp.zeros((pair_ids.shape[0], cos_lat.shape[0]), jnp.float32)
    packed = (slope.T, lagged.T, jnp.broadcast_to(restart_first, slope.shape).T, restart_second.T)
    _, values = lax.scan(advance, (empty, empty), packed, unroll=16)
    return jnp.transpose(values, (1, 0, 2))

def slot_table(row_map, owners, row_cap):
    onehot = (row_map[:, None] == jnp.arange(owners, dtype=jnp.int32)[None, :]).astype(jnp.int32)
    ranking = lax.optimization_barrier(jnp.sum((jnp.cumsum(onehot, axis=0) - onehot) * onehot, axis=1))
    slot_of_row = (row_map * row_cap + ranking).astype(jnp.int32)
    chosen = slot_of_row[None, :] == jnp.arange(owners * row_cap, dtype=jnp.int32)[:, None]
    return (slot_of_row, chosen)

def wave_order(wave_map, truncation):
    doubled = jnp.repeat(wave_map, 2)
    slots = jnp.arange(doubled.shape[0], dtype=jnp.int32)
    m_of_w = jnp.where(slots % 2 == 0, doubled, truncation - doubled).astype(jnp.int32)
    w_of_m = jnp.zeros_like(m_of_w).at[m_of_w].set(slots)
    return (m_of_w, w_of_m)

def fourier_tables(lengths, row_points, blocks):
    safe_len = jnp.maximum(lengths, 1).astype(jnp.int32)[:, None, None]
    step_angle = 2.0 * math.pi / safe_len.astype(jnp.float32)
    points = jnp.arange(row_points, dtype=jnp.int32)
    inside = points[None, :, None] < lengths[:, None, None]
    inner_m = jnp.arange(SUBW, dtype=jnp.int32)
    angles = (points[None, :, None] * inner_m[None, None, :] % safe_len).astype(jnp.float32) * step_angle
    cosine = jnp.where(inside, jnp.cos(angles), 0.0)
    sine_vals = jnp.where(inside, jnp.sin(angles), 0.0)
    trig_table = jnp.concatenate([jnp.concatenate([cosine, -sine_vals], axis=2), jnp.concatenate([sine_vals, cosine], axis=2)], axis=1)
    outer_m = jnp.arange(blocks, dtype=jnp.int32) * SUBW
    twists = (points[None, None, :] * outer_m[None, :, None] % safe_len).astype(jnp.float32) * step_angle
    return (rounded(trig_table), jnp.cos(twists), jnp.sin(twists))

def synthesize(coefficients, trig_table, twist_cos, twist_sin):
    waves_all = coefficients.shape[-1]
    weights = jnp.where(jnp.arange(waves_all) == 0, 1.0, 2.0)
    scaled = coefficients * weights
    leading = scaled.shape[:3] + (waves_all // SUBW, SUBW)
    stacked = jnp.concatenate([scaled[:, :, :, 0].reshape(leading), scaled[:, :, :, 1].reshape(leading)], axis=4)
    partial_h = jnp.einsum('rflqj,rkj->rflqk', stacked, trig_table, precision=lax.Precision.HIGHEST)
    row_points = twist_cos.shape[-1]
    return lax.optimization_barrier(jnp.sum(twist_cos[:, None, None] * partial_h[..., :row_points] - twist_sin[:, None, None] * partial_h[..., row_points:], axis=3))

def analyze(weighted, trig_table, twist_cos, twist_sin):
    spread = weighted[:, :, :, None, :]
    turned = rounded(jnp.concatenate([spread * twist_cos[:, None, None], -(spread * twist_sin[:, None, None])], axis=4))
    result = jnp.einsum('rflqk,rkj->rflqj', turned, trig_table, precision=lax.Precision.HIGHEST)
    leading = result.shape[:3] + (result.shape[3] * SUBW,)
    weights = jnp.where(jnp.arange(leading[3]) == 0, 1.0, 2.0)
    return rounded(jnp.stack([result[..., :SUBW].reshape(leading) * weights, result[..., SUBW:].reshape(leading) * weights], axis=3))

def reference(spec_in, observation_weight, latitude_row_length, wave_map, row_map):
    owners = N_BAND * N_LEV
    block_pairs = PAIRS // owners
    block_count = PAIRS // block_pairs
    blocks = WAVES // SUBW
    cos_lat, log_sin = latitudes(latitude_row_length, NHALF)
    slot_of_row, chosen = slot_table(row_map, owners, DEVICE_ROW_SLOTS)
    m_of_w, w_of_m = wave_order(wave_map, TRUNC)
    spectral_block_list = jnp.moveaxis(spec_in.astype(jnp.float32).reshape(2, 2, MODEL_LEVELS, block_count, block_pairs, NCOL), 3, 0)
    id_blocks = wave_map.reshape(block_count, block_pairs)

    def table_of(pair_ids):
        return rounded(legendre(pair_ids, cos_lat, log_sin, TRUNC))

    def synth_block(packed):
        pair_ids, spectra = packed
        sides = side_mask(pair_ids, TRUNC).astype(jnp.float32)
        return jnp.einsum('qnr,filqn,qns->rfliqs', table_of(pair_ids), spectra, sides, precision=lax.Precision.HIGHEST)
    fourier = lax.map(synth_block, (id_blocks, spectral_block_list))
    fourier = rounded(jnp.moveaxis(fourier, 0, 4).reshape(NLAT, 2, MODEL_LEVELS, 2, WAVES))
    coefficients = jnp.take(fourier, w_of_m, axis=4)

    def synth_row(packed):
        row_coef, length = packed
        trig_table, twist_cos, twist_sin = fourier_tables(length[None], LONGEST_ROW, blocks)
        return synthesize(row_coef[None], trig_table, twist_cos, twist_sin)[0]
    rows_grid = lax.map(synth_row, (coefficients, latitude_row_length))
    slot_row = lax.optimization_barrier(jnp.sum(jnp.where(chosen, jnp.arange(NLAT, dtype=jnp.int32)[None, :], 0), axis=1))
    filled = jnp.any(chosen, axis=1)
    grid_incr = jnp.where(filled[:, None, None, None], jnp.take(rows_grid, slot_row, axis=0), 0.0)
    weighted = grid_incr * observation_weight.astype(jnp.float32)[:, None]
    row_weighted = jnp.take(weighted, slot_of_row, axis=0)

    def analyze_row(packed):
        row_values, length = packed
        trig_table, twist_cos, twist_sin = fourier_tables(length[None], LONGEST_ROW, blocks)
        return analyze(row_values[None], trig_table, twist_cos, twist_sin)[0]
    back = lax.map(analyze_row, (row_weighted, latitude_row_length))
    back = jnp.take(back, m_of_w, axis=4).reshape(NLAT, 2, MODEL_LEVELS, 2, block_count, block_pairs, 2)
    back_blocks = jnp.moveaxis(back, 4, 0)
    normaliser = 1.0 / math.sqrt(NLAT * LONGEST_ROW)

    def adjoint_block(packed):
        pair_ids, rows_part = packed
        sides = side_mask(pair_ids, TRUNC).astype(jnp.float32)
        return jnp.einsum('qnr,rfliqs,qns->filqn', table_of(pair_ids), rows_part, sides, precision=lax.Precision.HIGHEST)
    gradient = lax.map(adjoint_block, (id_blocks, back_blocks))
    gradient = jnp.moveaxis(gradient, 0, 3).reshape(2, 2, MODEL_LEVELS, PAIRS, NCOL) * normaliser
    return (grid_incr, gradient.astype(jnp.bfloat16))
```

```python
import math

import jax
import jax.numpy as jnp
from jax import lax
from jax.experimental import pallas as pl
from jax.experimental.pallas import tpu as pltpu
from jax.sharding import PartitionSpec as P

SUBW = 128
LANES = 128
CHUNK = 144


def latitudes(latitude_row_length, halves):
    cycle_no = ((latitude_row_length - 16) // 4).astype(jnp.float32)
    colat = math.pi * (cycle_no - 0.25) / (2.0 * halves + 0.5)
    north = (
        jnp.arange(latitude_row_length.shape[0], dtype=jnp.int32)
        < latitude_row_length.shape[0] // 2
    )
    return (jnp.where(north, jnp.cos(colat), -jnp.cos(colat)), jnp.log(jnp.sin(colat)))


def diagonals(pair_ids, log_sin, truncation):
    first_order = pair_ids[:, None]
    counter = jnp.arange(1, truncation + 1, dtype=jnp.int32)
    log_terms = jnp.log(1.0 - 0.5 / counter.astype(jnp.float32))

    def start(orders):
        partial_sum = jnp.sum(
            jnp.where(counter[None, :] <= orders, log_terms[None, :], 0.0), axis=1, keepdims=True
        )
        order_m = orders.astype(jnp.float32)
        log_start = 0.5 * (jnp.log(order_m + 0.5) + partial_sum)
        return jnp.exp(log_start + order_m * log_sin[None, :])

    return (start(first_order), start(truncation - first_order))


def legendre_kernel(
    truncation, groups, group_pad, blocks, part, ids, spread, mu, diag1, diag2, bound, out,
    slopes, laggeds, values, newer, older,
):
    step = pl.program_id(0)
    half = groups // blocks

    @pl.when(step == 0)
    def _():
        newer[...] = jnp.zeros_like(newer)
        older[...] = diag1[...]

    column = lax.broadcasted_iota(jnp.int32, (CHUNK, 256), 0) + step * CHUNK
    lane = lax.broadcasted_iota(jnp.int32, (CHUNK, 256), 1)

    def split(x):
        high = x.astype(jnp.bfloat16).astype(jnp.float32)
        rest = x - high
        middle = rest.astype(jnp.bfloat16).astype(jnp.float32)
        low = rest - middle
        piece = jnp.where(lane < part, high, jnp.where(lane < 2 * part, middle, low))
        return piece.astype(jnp.bfloat16)

    for b in range(blocks):
        first_order = ids[b : b + 1, :]
        boundary = truncation + 1 - first_order
        first_side = column < boundary
        order_m = jnp.where(first_side, first_order, truncation - first_order).astype(jnp.float32)
        degree = jnp.where(first_side, first_order + column, column - 1).astype(jnp.float32)
        restart_first = column == 0
        restart = restart_first | (column == boundary)

        def epsilon(v):
            upper = jnp.maximum(v * v - order_m * order_m, 0.0)
            lower = jnp.maximum(4.0 * v * v - 1.0, 1.0)
            return jnp.sqrt(upper / lower)

        inverse = 1.0 / jnp.where(restart, 1.0, epsilon(degree))
        slope = jnp.where(restart, 0.0, inverse)
        lagged = jnp.where(restart, 0.0, -epsilon(degree - 1.0) * inverse)
        lagged = jnp.where(restart_first, 1.0, lagged)
        for table, compact in ((slopes, slope), (laggeds, lagged)):
            wide = jnp.dot(split(compact), spread[...], preferred_element_type=jnp.float32)
            for g in range(half):
                table[pl.ds(b * half + g, CHUNK, stride=group_pad), :] = wide[
                    :, g * LANES : (g + 1) * LANES
                ]

    mu_v = mu[...]
    diag2_v = diag2[...]
    bound_v = bound[...]

    def advance(i, carry):
        new, old = carry
        rows = pl.ds(pl.multiple_of(i * group_pad, 8), group_pad)
        lag = jnp.where(bound_v == step * CHUNK + i, diag2_v, laggeds[rows, :] * old)
        value = slopes[rows, :] * mu_v * new + lag
        values[rows, :] = value
        return (value, new)

    new, old = lax.fori_loop(0, CHUNK, advance, (newer[...], older[...]), unroll=16)
    newer[...] = new
    older[...] = old
    for g in range(groups):
        out[g] = values[pl.ds(g, CHUNK, stride=group_pad), :].astype(jnp.bfloat16)


def legendre(pair_ids, cos_lat, log_sin, truncation):
    pairs = pair_ids.shape[0]
    rows = cos_lat.shape[0]
    groups = pairs * rows // LANES
    group_pad = -(-groups // 8) * 8
    blocks = -(-pairs // 80)
    part = pairs // blocks
    chunks = -(-(truncation + 2) // CHUNK)
    diag1, diag2 = diagonals(pair_ids, log_sin, truncation)

    def lay(x):
        x = jnp.broadcast_to(x, (pairs, rows)).reshape(groups, LANES)
        return jnp.pad(x, ((0, group_pad - groups), (0, 0)))

    ids = jnp.tile(pair_ids.reshape(blocks, part), (1, 3))
    ids = jnp.pad(ids, ((0, 0), (0, 256 - 3 * part)))
    source = jnp.arange(256, dtype=jnp.int32)[:, None]
    target = jnp.arange(part * rows, dtype=jnp.int32)[None, :] // rows
    spread = ((source % part == target) & (source < 3 * part)).astype(jnp.bfloat16)
    whole = pl.BlockSpec(memory_space=pltpu.VMEM)
    tall = pltpu.VMEM((CHUNK * group_pad, LANES), jnp.float32)
    state = pltpu.VMEM((group_pad, LANES), jnp.float32)

    def kernel(*refs):
        legendre_kernel(truncation, groups, group_pad, blocks, part, *refs)

    return pl.pallas_call(
        kernel,
        grid=(chunks,),
        in_specs=[whole] * 6,
        out_specs=pl.BlockSpec((groups, CHUNK, LANES), lambda i: (0, i, 0)),
        out_shape=jax.ShapeDtypeStruct((groups, chunks * CHUNK, LANES), jnp.bfloat16),
        scratch_shapes=[tall, tall, tall, state, state],
        compiler_params=pltpu.CompilerParams(vmem_limit_bytes=48 * 2**20),
        name="legendre",
    )(
        ids,
        spread,
        lay(cos_lat[None, :]),
        lay(diag1),
        lay(diag2),
        lay(truncation + 1 - pair_ids[:, None]),
    )


def slot_table(row_map, owners, row_cap):
    onehot = (row_map[:, None] == jnp.arange(owners, dtype=jnp.int32)[None, :]).astype(jnp.int32)
    ranking = jnp.sum((jnp.cumsum(onehot, axis=0) - onehot) * onehot, axis=1)
    slot_of_row = row_map * row_cap + ranking
    return slot_of_row[None, :] == jnp.arange(owners * row_cap, dtype=jnp.int32)[:, None]


def angle_tables(lengths, orders, points):
    safe_len = jnp.maximum(lengths, 1)[:, None, None]
    step_angle = 2.0 * math.pi / safe_len.astype(jnp.float32)
    angles = (points[None, :, None] * orders[None, None, :] % safe_len).astype(
        jnp.float32
    ) * step_angle
    return jnp.cos(angles), jnp.sin(angles)


def fourier_tables(lengths, high_count, blocks):
    low = jnp.arange(LANES, dtype=jnp.int32)
    high = jnp.arange(high_count, dtype=jnp.int32) * LANES
    inner = jnp.arange(SUBW, dtype=jnp.int32)
    outer = jnp.arange(blocks, dtype=jnp.int32) * SUBW
    slots = lengths.shape[0]
    low_c, low_s = (x[:, None] for x in angle_tables(lengths, inner, low))
    high_c, high_s = (x[:, :, None] for x in angle_tables(lengths, inner, high))
    shape = (slots, high_count * LANES, SUBW)
    cosine = (low_c * high_c - low_s * high_s).astype(jnp.bfloat16).reshape(shape)
    sine = (low_s * high_c + low_c * high_s).astype(jnp.bfloat16).reshape(shape)
    low_c, low_s = (x[:, :, None] for x in angle_tables(lengths, low, outer))
    high_c, high_s = (x[:, :, :, None] for x in angle_tables(lengths, high, outer))
    shape = (slots, blocks, high_count * LANES)
    twist_cos = (low_c * high_c - low_s * high_s).reshape(shape)
    twist_sin = (low_s * high_c + low_c * high_s).reshape(shape)
    return cosine, sine, twist_cos, twist_sin


def body(spec_in, observation_weight, latitude_row_length, wave_map, row_map):
    bands = lax.axis_size("band")
    levels = lax.axis_size("lev")
    owners = bands * levels
    owner_index = lax.axis_index("band") * levels + lax.axis_index("lev")
    columns = spec_in.shape[4]
    truncation = columns - 2
    waves_all = truncation + 1
    blocks = waves_all // SUBW
    row_cap = observation_weight.shape[0]
    row_points = observation_weight.shape[2]
    rows = latitude_row_length.shape[0]
    pairs = spec_in.shape[3]
    grouped = LANES // rows
    groups = pairs // grouped
    cos_lat, log_sin = latitudes(latitude_row_length, (row_points - 16) // 4)
    pair_ids = lax.dynamic_slice_in_dim(wave_map, lax.axis_index("band") * pairs, pairs)
    functions = legendre(pair_ids, cos_lat, log_sin, truncation)[:, :columns]
    own = jnp.eye(grouped, dtype=jnp.float32)[None, None, None, None, :, :, None]

    first_side = (
        jnp.arange(columns, dtype=jnp.int32)[None, :] < truncation + 1 - pair_ids[:, None]
    )
    sides = jnp.stack([first_side, jnp.logical_not(first_side)]).astype(jnp.bfloat16)
    masked = spec_in[None, :, :, 0] * sides[:, None, None]
    masked = masked.reshape(2, 2, 2, groups, grouped, columns)
    product = jnp.einsum(
        "gnx,sfigcn->gsficx", functions, masked, preferred_element_type=jnp.float32
    )
    product = product.reshape(groups, 2, 2, 2, grouped, grouped, rows)
    fourier = jnp.sum(product * own, axis=5).astype(jnp.bfloat16)
    fourier = jnp.transpose(fourier, (5, 2, 3, 0, 4, 1)).reshape(rows, -1)

    chosen = slot_table(row_map, owners, row_cap)
    picker = chosen.astype(jnp.bfloat16)
    outgoing = jnp.dot(picker, fourier, preferred_element_type=jnp.float32).astype(jnp.bfloat16)
    outgoing = outgoing.reshape(owners, row_cap * 4, 2 * pairs)
    arrived = lax.all_to_all(outgoing, ("band", "lev"), split_axis=0, concat_axis=0, tiled=True)
    arrived = arrived.reshape(bands, levels, row_cap, 2, 2, 2 * pairs)
    arrived = jnp.transpose(arrived, (2, 3, 1, 4, 0, 5)).reshape(-1, waves_all)
    doubled = jnp.repeat(wave_map, 2)
    odd = jnp.arange(waves_all, dtype=jnp.int32) % 2
    m_of_w = jnp.where(odd == 0, doubled, truncation - doubled)
    order = jnp.arange(waves_all, dtype=jnp.int32)
    gain = jnp.where(order == 0, 1.0, 2.0)
    permute = jnp.where(m_of_w[:, None] == order[None, :], gain[None, :], 0.0).astype(jnp.bfloat16)
    scaled = jnp.dot(arrived, permute, preferred_element_type=jnp.float32).astype(jnp.bfloat16)
    scaled = scaled.reshape(row_cap, 2, levels, 2, blocks, SUBW)

    slot_length = jnp.sum(jnp.where(chosen, latitude_row_length[None, :], 0), axis=1)
    lengths = lax.dynamic_slice_in_dim(slot_length, owner_index * row_cap, row_cap)
    high_count = -(-row_points // LANES)
    cosine, sine, twist_cos, twist_sin = fourier_tables(lengths, high_count, blocks)
    stacked = jnp.concatenate([scaled[:, :, :, 0], scaled[:, :, :, 1]], axis=4)
    table_re = jnp.concatenate([cosine, -sine], axis=2)
    table_im = jnp.concatenate([sine, cosine], axis=2)
    half_re = jnp.einsum("rflqj,rkj->rflqk", stacked, table_re, preferred_element_type=jnp.float32)
    half_im = jnp.einsum("rflqj,rkj->rflqk", stacked, table_im, preferred_element_type=jnp.float32)
    spread_cos = twist_cos[:, None, None]
    spread_sin = twist_sin[:, None, None]
    grid = jnp.sum(spread_cos * half_re - spread_sin * half_im, axis=3)
    inside = jnp.arange(high_count * LANES, dtype=jnp.int32)[None, :] < lengths[:, None]
    grid = jnp.where(inside[:, None, None], grid, 0.0)
    grid_incr = grid[..., :row_points]

    weight = jnp.pad(
        observation_weight.astype(jnp.float32), ((0, 0), (0, 0), (0, high_count * LANES - row_points))
    )
    weighted = (grid * weight[:, None])[:, :, :, None]
    turned_re = (weighted * spread_cos).astype(jnp.bfloat16)
    turned_im = (-(weighted * spread_sin)).astype(jnp.bfloat16)
    result = jnp.einsum(
        "rflqk,rkj->rflqj", turned_re, table_re, preferred_element_type=jnp.float32
    ) + jnp.einsum("rflqk,rkj->rflqj", turned_im, table_im, preferred_element_type=jnp.float32)
    back = jnp.stack([result[..., :SUBW], result[..., SUBW:]], axis=3).astype(jnp.bfloat16)
    back = back.reshape(-1, waves_all)
    back = lax.dot_general(
        back, permute, (((1,), (1,)), ((), ())), preferred_element_type=jnp.float32
    ).astype(jnp.bfloat16)
    back = back.reshape(row_cap, 2, levels, 2, bands, 2 * pairs)
    returning = jnp.transpose(back, (4, 2, 0, 1, 3, 5)).reshape(owners, row_cap * 4, 2 * pairs)
    returned = lax.all_to_all(returning, ("band", "lev"), split_axis=0, concat_axis=0, tiled=True)
    by_row = jnp.dot(
        picker.T, returned.reshape(owners * row_cap, -1), preferred_element_type=jnp.float32
    ).astype(jnp.bfloat16)
    by_row = by_row.reshape(rows, 2, 2, groups, grouped, 2)
    by_row = jnp.transpose(by_row, (3, 5, 1, 2, 4, 0))[:, :, :, :, :, None]
    spread_rows = (by_row * own.astype(jnp.bfloat16)).reshape(groups, 2, 2, 2, grouped, LANES)
    gradient = jnp.einsum(
        "gsficx,gnx->sfigcn", spread_rows, functions, preferred_element_type=jnp.float32
    ).reshape(2, 2, 2, pairs, columns)
    normaliser = 1.0 / math.sqrt(rows * row_points)
    gradient = jnp.where(first_side, gradient[0], gradient[1]) * normaliser
    return (grid_incr, gradient.astype(jnp.bfloat16)[:, :, None])


def solution(mesh):
    return jax.shard_map(
        body,
        mesh=mesh,
        in_specs=(
            P("member", None, "lev", "band", None),
            P(("band", "lev"), "member", None),
            P(),
            P(),
            P(),
        ),
        out_specs=(
            P(("band", "lev"), None, "member", None),
            P("member", None, "lev", "band", None),
        ),
        check_vma=False,
    )
```

```python
import math

import jax
import jax.numpy as jnp
from jax import lax
from jax.experimental import pallas as pl
from jax.experimental.pallas import tpu as pltpu
from jax.sharding import PartitionSpec as P

SUBW = 128
LANES = 128
CHUNK = 144


def latitudes(latitude_row_length, halves):
    cycle_no = ((latitude_row_length - 16) // 4).astype(jnp.float32)
    colat = math.pi * (cycle_no - 0.25) / (2.0 * halves + 0.5)
    north = (
        jnp.arange(latitude_row_length.shape[0], dtype=jnp.int32)
        < latitude_row_length.shape[0] // 2
    )
    return (jnp.where(north, jnp.cos(colat), -jnp.cos(colat)), jnp.log(jnp.sin(colat)))


def diagonals(pair_ids, log_sin, truncation):
    first_order = pair_ids[:, None]
    counter = jnp.arange(1, truncation + 1, dtype=jnp.int32)
    log_terms = jnp.log(1.0 - 0.5 / counter.astype(jnp.float32))

    def start(orders):
        partial_sum = jnp.sum(
            jnp.where(counter[None, :] <= orders, log_terms[None, :], 0.0), axis=1, keepdims=True
        )
        order_m = orders.astype(jnp.float32)
        log_start = 0.5 * (jnp.log(order_m + 0.5) + partial_sum)
        return jnp.exp(log_start + order_m * log_sin[None, :])

    return (start(first_order), start(truncation - first_order))


def legendre_kernel(
    truncation, groups, group_pad, blocks, part, cluster, ids, spread, mu, diag1, diag2, bound,
    limit, own, spec, out, fourier, slopes, laggeds, values, newer, older, kept,
):
    step = pl.program_id(0)
    half = groups // blocks
    wide_lanes = kept.shape[2]
    tiles = wide_lanes // LANES

    @pl.when(step == 0)
    def _():
        newer[...] = jnp.zeros_like(newer)
        older[...] = diag1[...]

    column = lax.broadcasted_iota(jnp.int32, (CHUNK, 256), 0) + step * CHUNK
    lane = lax.broadcasted_iota(jnp.int32, (CHUNK, 256), 1)

    def split(x):
        high = x.astype(jnp.bfloat16).astype(jnp.float32)
        rest = x - high
        middle = rest.astype(jnp.bfloat16).astype(jnp.float32)
        low = rest - middle
        piece = jnp.where(lane < part, high, jnp.where(lane < 2 * part, middle, low))
        return piece.astype(jnp.bfloat16)

    for b in range(blocks):
        first_order = ids[b : b + 1, :]
        boundary = truncation + 1 - first_order
        first_side = column < boundary
        order_m = jnp.where(first_side, first_order, truncation - first_order).astype(jnp.float32)
        degree = jnp.where(first_side, first_order + column, column - 1).astype(jnp.float32)
        restart_first = column == 0
        restart = restart_first | (column == boundary)

        def squared(v):
            upper = jnp.maximum(v * v - order_m * order_m, 0.0)
            lower = jnp.maximum(4.0 * v * v - 1.0, 1.0)
            return upper / lower

        inverse = lax.rsqrt(jnp.where(restart, 1.0, squared(degree)))
        slope = jnp.where(restart, 0.0, inverse)
        lagged = jnp.where(restart, 0.0, -jnp.sqrt(squared(degree - 1.0)) * inverse)
        lagged = jnp.where(restart_first, 1.0, lagged)
        for table, compact in ((slopes, slope), (laggeds, lagged)):
            wide = jnp.dot(split(compact), spread[...], preferred_element_type=jnp.float32)
            for g in range(half):
                table[pl.ds(b * half + g, CHUNK, stride=group_pad), :] = wide[
                    :, g * LANES : (g + 1) * LANES
                ]

    mu_v = mu[...]
    diag2_v = diag2[...]
    bound_v = bound[...]

    def advance(i, carry):
        new, old = carry
        rows = pl.ds(pl.multiple_of(i * group_pad, 8), group_pad)
        lag = jnp.where(bound_v == step * CHUNK + i, diag2_v, laggeds[rows, :] * old)
        value = slopes[rows, :] * mu_v * new + lag
        values[rows, :] = value
        return (value, new)

    new, old = lax.fori_loop(0, CHUNK, advance, (newer[...], older[...]), unroll=16)
    newer[...] = new
    older[...] = old
    here = pl.ds(pl.multiple_of(step * CHUNK, CHUNK), CHUNK)
    for g in range(groups):
        piece = values[pl.ds(g, CHUNK, stride=group_pad), :].astype(jnp.bfloat16)
        lanes = pl.ds((g % tiles) * LANES, LANES)
        out[g // tiles, :, lanes] = piece
        kept[g // tiles, here, lanes] = piece

    @pl.when(step == pl.num_programs(0) - 1)
    def _():
        columns = spec.shape[3]
        point = lax.broadcasted_iota(jnp.int32, (cluster, columns), 1)
        for k in range(groups // tiles):
            pairs = pl.ds(k * cluster, cluster)
            first = jnp.where(point < limit[pairs, :], 1.0, 0.0).astype(jnp.bfloat16)
            table = kept[k, :columns, :]
            operands = []
            for f in range(2):
                for i in range(2):
                    x = spec[f, i, pairs, :]
                    y = x * first
                    operands += [y, x - y]
            product = jnp.dot(
                jnp.concatenate(operands, axis=0), table, preferred_element_type=jnp.float32
            )
            product = product.reshape(8, cluster, wide_lanes) * own[...][None]
            fourier[k] = jnp.sum(product, axis=1)


def adjoint_kernel(cluster, normaliser, limit, own, back, table, out):
    columns = out.shape[3]
    mask = own[...]
    rows = back[0]
    operands = [mask * rows[x : x + 1, :] for x in range(8)]
    result = lax.dot_general(
        jnp.concatenate(operands, axis=0).astype(jnp.bfloat16),
        table[0],
        (((1,), (1,)), ((), ())),
        preferred_element_type=jnp.float32,
    )
    first = lax.broadcasted_iota(jnp.int32, (cluster, columns), 1) < limit[...]
    for x in range(4):
        one = result[2 * x * cluster : (2 * x + 1) * cluster, :columns]
        two = result[(2 * x + 1) * cluster : (2 * x + 2) * cluster, :columns]
        out[x // 2, x % 2] = (jnp.where(first, one, two) * normaliser).astype(jnp.bfloat16)


def cluster_of(pairs):
    return 16 if pairs % 16 == 0 else pairs


def own_mask(cluster, rows):
    lane = jnp.arange(cluster * rows, dtype=jnp.int32)[None, :] // rows
    return (lane == jnp.arange(cluster, dtype=jnp.int32)[:, None]).astype(jnp.float32)


def legendre(spec, pair_ids, cos_lat, log_sin, truncation):
    pairs = pair_ids.shape[0]
    rows = cos_lat.shape[0]
    groups = pairs * rows // LANES
    group_pad = -(-groups // 8) * 8
    blocks = -(-pairs // 80)
    part = pairs // blocks
    cluster = cluster_of(pairs)
    clusters = pairs // cluster
    wide = cluster * rows
    chunks = -(-(truncation + 2) // CHUNK)
    diag1, diag2 = diagonals(pair_ids, log_sin, truncation)

    def lay(x):
        x = jnp.broadcast_to(x, (pairs, rows)).reshape(groups, LANES)
        return jnp.pad(x, ((0, group_pad - groups), (0, 0)))

    ids = jnp.tile(pair_ids.reshape(blocks, part), (1, 3))
    ids = jnp.pad(ids, ((0, 0), (0, 256 - 3 * part)))
    source = jnp.arange(256, dtype=jnp.int32)[:, None]
    target = jnp.arange(part * rows, dtype=jnp.int32)[None, :] // rows
    spread = ((source % part == target) & (source < 3 * part)).astype(jnp.bfloat16)
    whole = pl.BlockSpec(memory_space=pltpu.VMEM)
    tall = pltpu.VMEM((CHUNK * group_pad, LANES), jnp.float32)
    state = pltpu.VMEM((group_pad, LANES), jnp.float32)
    limit = truncation + 1 - pair_ids[:, None]

    def kernel(*refs):
        legendre_kernel(truncation, groups, group_pad, blocks, part, cluster, *refs)

    return pl.pallas_call(
        kernel,
        grid=(chunks,),
        in_specs=[whole] * 9,
        out_specs=(pl.BlockSpec((clusters, CHUNK, wide), lambda i: (0, i, 0)), whole),
        out_shape=(
            jax.ShapeDtypeStruct((clusters, chunks * CHUNK, wide), jnp.bfloat16),
            jax.ShapeDtypeStruct((clusters, 8, wide), jnp.float32),
        ),
        scratch_shapes=[
            tall, tall, tall, state, state,
            pltpu.VMEM((clusters, chunks * CHUNK, wide), jnp.bfloat16),
        ],
        compiler_params=pltpu.CompilerParams(vmem_limit_bytes=58 * 2**20),
        name="legendre",
    )(
        ids, spread, lay(cos_lat[None, :]), lay(diag1), lay(diag2), lay(limit), limit,
        own_mask(cluster, rows), spec,
    )


def adjoint(back, table, pair_ids, rows, columns, normaliser):
    pairs = pair_ids.shape[0]
    cluster = cluster_of(pairs)
    wide = cluster * rows
    limit = columns - 1 - pair_ids[:, None]

    def kernel(*refs):
        adjoint_kernel(cluster, normaliser, *refs)

    return pl.pallas_call(
        kernel,
        grid=(pairs // cluster,),
        in_specs=[
            pl.BlockSpec((cluster, 1), lambda i: (i, 0)),
            pl.BlockSpec((cluster, wide), lambda i: (0, 0)),
            pl.BlockSpec((1, 8, wide), lambda i: (i, 0, 0)),
            pl.BlockSpec((1, table.shape[1], wide), lambda i: (i, 0, 0)),
        ],
        out_specs=pl.BlockSpec((2, 2, cluster, columns), lambda i: (0, 0, i, 0)),
        out_shape=jax.ShapeDtypeStruct((2, 2, pairs, columns), jnp.bfloat16),
        compiler_params=pltpu.CompilerParams(vmem_limit_bytes=58 * 2**20),
        name="adjoint",
    )(limit, own_mask(cluster, rows), back, table)


def slot_table(row_map, owners, row_cap):
    onehot = (row_map[:, None] == jnp.arange(owners, dtype=jnp.int32)[None, :]).astype(jnp.int32)
    ranking = jnp.sum((jnp.cumsum(onehot, axis=0) - onehot) * onehot, axis=1)
    slot_of_row = row_map * row_cap + ranking
    return slot_of_row[None, :] == jnp.arange(owners * row_cap, dtype=jnp.int32)[:, None]


def angle_tables(lengths, orders, points):
    safe_len = jnp.maximum(lengths, 1)[:, None, None]
    step_angle = 2.0 * math.pi / safe_len.astype(jnp.float32)
    angles = (points[None, :, None] * orders[None, None, :] % safe_len).astype(
        jnp.float32
    ) * step_angle
    return jnp.cos(angles), jnp.sin(angles)


def fourier_tables(lengths, high_count, blocks):
    low = jnp.arange(LANES, dtype=jnp.int32)
    high = jnp.arange(high_count, dtype=jnp.int32) * LANES
    inner = jnp.arange(SUBW, dtype=jnp.int32)
    outer = jnp.arange(blocks, dtype=jnp.int32) * SUBW
    slots = lengths.shape[0]
    low_c, low_s = (x[:, None] for x in angle_tables(lengths, inner, low))
    high_c, high_s = (x[:, :, None] for x in angle_tables(lengths, inner, high))
    shape = (slots, high_count * LANES, SUBW)
    cosine = (low_c * high_c - low_s * high_s).astype(jnp.bfloat16).reshape(shape)
    sine = (low_s * high_c + low_c * high_s).astype(jnp.bfloat16).reshape(shape)
    low_c, low_s = (x[:, :, None] for x in angle_tables(lengths, low, outer))
    high_c, high_s = (x[:, :, :, None] for x in angle_tables(lengths, high, outer))
    shape = (slots, blocks, high_count * LANES)
    twist_cos = (low_c * high_c - low_s * high_s).reshape(shape)
    twist_sin = (low_s * high_c + low_c * high_s).reshape(shape)
    return cosine, sine, twist_cos, twist_sin


def body(spec_in, observation_weight, latitude_row_length, wave_map, row_map):
    bands = lax.axis_size("band")
    levels = lax.axis_size("lev")
    owners = bands * levels
    owner_index = lax.axis_index("band") * levels + lax.axis_index("lev")
    columns = spec_in.shape[4]
    truncation = columns - 2
    waves_all = truncation + 1
    blocks = waves_all // SUBW
    row_cap = observation_weight.shape[0]
    row_points = observation_weight.shape[2]
    rows = latitude_row_length.shape[0]
    pairs = spec_in.shape[3]
    cos_lat, log_sin = latitudes(latitude_row_length, (row_points - 16) // 4)
    pair_ids = lax.dynamic_slice_in_dim(wave_map, lax.axis_index("band") * pairs, pairs)
    functions, fourier = legendre(spec_in[:, :, 0], pair_ids, cos_lat, log_sin, truncation)
    clusters = functions.shape[0]
    cluster = pairs // clusters
    fourier = fourier.astype(jnp.bfloat16).reshape(clusters, 2, 2, 2, cluster, rows)
    fourier = jnp.transpose(fourier, (5, 1, 2, 0, 4, 3)).reshape(rows, -1)

    chosen = slot_table(row_map, owners, row_cap)
    picker = chosen.astype(jnp.bfloat16)
    outgoing = jnp.dot(picker, fourier, preferred_element_type=jnp.float32).astype(jnp.bfloat16)
    outgoing = outgoing.reshape(owners, row_cap * 4, 2 * pairs)
    arrived = lax.all_to_all(outgoing, ("band", "lev"), split_axis=0, concat_axis=0, tiled=True)
    arrived = arrived.reshape(bands, levels, row_cap, 2, 2, 2 * pairs)
    arrived = jnp.transpose(arrived, (2, 3, 1, 4, 0, 5)).reshape(-1, waves_all)
    doubled = jnp.repeat(wave_map, 2)
    odd = jnp.arange(waves_all, dtype=jnp.int32) % 2
    m_of_w = jnp.where(odd == 0, doubled, truncation - doubled)
    order = jnp.arange(waves_all, dtype=jnp.int32)
    gain = jnp.where(order == 0, 1.0, 2.0)
    permute = jnp.where(m_of_w[:, None] == order[None, :], gain[None, :], 0.0).astype(jnp.bfloat16)
    scaled = jnp.dot(arrived, permute, preferred_element_type=jnp.float32).astype(jnp.bfloat16)
    scaled = scaled.reshape(row_cap, 2, levels, 2, blocks, SUBW)

    slot_length = jnp.sum(jnp.where(chosen, latitude_row_length[None, :], 0), axis=1)
    lengths = lax.dynamic_slice_in_dim(slot_length, owner_index * row_cap, row_cap)
    high_count = -(-row_points // LANES)
    cosine, sine, twist_cos, twist_sin = fourier_tables(lengths, high_count, blocks)
    stacked = jnp.concatenate([scaled[:, :, :, 0], scaled[:, :, :, 1]], axis=4)
    table_re = jnp.concatenate([cosine, -sine], axis=2)
    table_im = jnp.concatenate([sine, cosine], axis=2)
    half_re = jnp.einsum("rflqj,rkj->rflqk", stacked, table_re, preferred_element_type=jnp.float32)
    half_im = jnp.einsum("rflqj,rkj->rflqk", stacked, table_im, preferred_element_type=jnp.float32)
    spread_cos = twist_cos[:, None, None]
    spread_sin = twist_sin[:, None, None]
    grid = jnp.sum(spread_cos * half_re - spread_sin * half_im, axis=3)
    inside = jnp.arange(high_count * LANES, dtype=jnp.int32)[None, :] < lengths[:, None]
    grid = jnp.where(inside[:, None, None], grid, 0.0)
    grid_incr = grid[..., :row_points]

    weight = jnp.pad(
        observation_weight.astype(jnp.float32), ((0, 0), (0, 0), (0, high_count * LANES - row_points))
    )
    weighted = (grid * weight[:, None])[:, :, :, None]
    turned_re = (weighted * spread_cos).astype(jnp.bfloat16)
    turned_im = (-(weighted * spread_sin)).astype(jnp.bfloat16)
    result = jnp.einsum(
        "rflqk,rkj->rflqj", turned_re, table_re, preferred_element_type=jnp.float32
    ) + jnp.einsum("rflqk,rkj->rflqj", turned_im, table_im, preferred_element_type=jnp.float32)
    back = jnp.stack([result[..., :SUBW], result[..., SUBW:]], axis=3).astype(jnp.bfloat16)
    back = back.reshape(-1, waves_all)
    back = lax.dot_general(
        back, permute, (((1,), (1,)), ((), ())), preferred_element_type=jnp.float32
    ).astype(jnp.bfloat16)
    back = back.reshape(row_cap, 2, levels, 2, bands, 2 * pairs)
    returning = jnp.transpose(back, (4, 2, 0, 1, 3, 5)).reshape(owners, row_cap * 4, 2 * pairs)
    returned = lax.all_to_all(returning, ("band", "lev"), split_axis=0, concat_axis=0, tiled=True)
    by_row = jnp.dot(
        picker.T, returned.reshape(owners * row_cap, -1), preferred_element_type=jnp.float32
    ).astype(jnp.bfloat16)
    by_row = by_row.reshape(rows, 2, 2, clusters, cluster, 2)
    by_row = jnp.transpose(by_row, (3, 1, 2, 5, 4, 0)).reshape(clusters, 8, cluster * rows)
    normaliser = 1.0 / math.sqrt(rows * row_points)
    gradient = adjoint(
        by_row.astype(jnp.float32), functions, pair_ids, rows, columns, normaliser
    )
    return (grid_incr, gradient[:, :, None])


def solution(mesh):
    return jax.shard_map(
        body,
        mesh=mesh,
        in_specs=(
            P("member", None, "lev", "band", None),
            P(("band", "lev"), "member", None),
            P(),
            P(),
            P(),
        ),
        out_specs=(
            P(("band", "lev"), None, "member", None),
            P("member", None, "lev", "band", None),
        ),
        check_vma=False,
    )
```

```python
import math

import jax
import jax.numpy as jnp
from jax import lax
from jax.experimental import pallas as pl
from jax.experimental.pallas import tpu as pltpu
from jax.sharding import PartitionSpec as P

SUBW = 128
LANES = 128
CHUNK = 144


def latitudes(latitude_row_length, halves):
    cycle_no = ((latitude_row_length - 16) // 4).astype(jnp.float32)
    colat = math.pi * (cycle_no - 0.25) / (2.0 * halves + 0.5)
    north = (
        jnp.arange(latitude_row_length.shape[0], dtype=jnp.int32)
        < latitude_row_length.shape[0] // 2
    )
    return (jnp.where(north, jnp.cos(colat), -jnp.cos(colat)), jnp.log(jnp.sin(colat)))


def diagonals(pair_ids, log_sin, truncation):
    first_order = pair_ids[:, None]
    counter = jnp.arange(1, truncation + 1, dtype=jnp.int32)
    log_terms = jnp.log(1.0 - 0.5 / counter.astype(jnp.float32))

    def start(orders):
        partial_sum = jnp.sum(
            jnp.where(counter[None, :] <= orders, log_terms[None, :], 0.0), axis=1, keepdims=True
        )
        order_m = orders.astype(jnp.float32)
        log_start = 0.5 * (jnp.log(order_m + 0.5) + partial_sum)
        return jnp.exp(log_start + order_m * log_sin[None, :])

    return (start(first_order), start(truncation - first_order))


def legendre_kernel(
    truncation, groups, group_pad, blocks, part, cluster, ids, spread, mu, diag1, diag2, bound,
    limit, own, spec, out, fourier, slopes, laggeds, values, newer, older, kept,
):
    step = pl.program_id(0)
    half = groups // blocks
    wide_lanes = kept.shape[2]
    tiles = wide_lanes // LANES

    @pl.when(step == 0)
    def _():
        newer[...] = jnp.zeros_like(newer)
        older[...] = diag1[...]

    column = lax.broadcasted_iota(jnp.int32, (CHUNK, 256), 0) + step * CHUNK
    lane = lax.broadcasted_iota(jnp.int32, (CHUNK, 256), 1)

    def split(x):
        high = x.astype(jnp.bfloat16).astype(jnp.float32)
        rest = x - high
        middle = rest.astype(jnp.bfloat16).astype(jnp.float32)
        low = rest - middle
        piece = jnp.where(lane < part, high, jnp.where(lane < 2 * part, middle, low))
        return piece.astype(jnp.bfloat16)

    for b in range(blocks):
        first_order = ids[b : b + 1, :]
        boundary = truncation + 1 - first_order
        first_side = column < boundary
        order_m = jnp.where(first_side, first_order, truncation - first_order).astype(jnp.float32)
        degree = jnp.where(first_side, first_order + column, column - 1).astype(jnp.float32)
        restart_first = column == 0
        restart = restart_first | (column == boundary)

        def squared(v):
            upper = jnp.maximum(v * v - order_m * order_m, 0.0)
            lower = jnp.maximum(4.0 * v * v - 1.0, 1.0)
            return upper / lower

        inverse = lax.rsqrt(jnp.where(restart, 1.0, squared(degree)))
        slope = jnp.where(restart, 0.0, inverse)
        lagged = jnp.where(restart, 0.0, -jnp.sqrt(squared(degree - 1.0)) * inverse)
        lagged = jnp.where(restart_first, 1.0, lagged)
        for table, compact in ((slopes, slope), (laggeds, lagged)):
            wide = jnp.dot(split(compact), spread[...], preferred_element_type=jnp.float32)
            for g in range(half):
                table[pl.ds(b * half + g, CHUNK, stride=group_pad), :] = wide[
                    :, g * LANES : (g + 1) * LANES
                ]

    mu_v = mu[...]
    diag2_v = diag2[...]
    bound_v = bound[...]

    def advance(i, carry):
        new, old = carry
        rows = pl.ds(pl.multiple_of(i * group_pad, 8), group_pad)
        lag = jnp.where(bound_v == step * CHUNK + i, diag2_v, laggeds[rows, :] * old)
        value = slopes[rows, :] * mu_v * new + lag
        values[rows, :] = value
        return (value, new)

    new, old = lax.fori_loop(0, CHUNK, advance, (newer[...], older[...]), unroll=16)
    newer[...] = new
    older[...] = old
    here = pl.ds(pl.multiple_of(step * CHUNK, CHUNK), CHUNK)
    for g in range(groups):
        piece = values[pl.ds(g, CHUNK, stride=group_pad), :].astype(jnp.bfloat16)
        lanes = pl.ds((g % tiles) * LANES, LANES)
        out[g // tiles, :, lanes] = piece
        kept[g // tiles, here, lanes] = piece

    @pl.when(step == pl.num_programs(0) - 1)
    def _():
        columns = spec.shape[3]
        point = lax.broadcasted_iota(jnp.int32, (cluster, columns), 1)
        for k in range(groups // tiles):
            pairs = pl.ds(k * cluster, cluster)
            first = jnp.where(point < limit[pairs, :], 1.0, 0.0).astype(jnp.bfloat16)
            table = kept[k, :columns, :]
            operands = []
            for f in range(2):
                for i in range(2):
                    x = spec[f, i, pairs, :]
                    y = x * first
                    operands += [y, x - y]
            product = jnp.dot(
                jnp.concatenate(operands, axis=0), table, preferred_element_type=jnp.float32
            )
            product = product.reshape(8, cluster, wide_lanes) * own[...][None]
            fourier[k] = jnp.sum(product, axis=1)


def adjoint_kernel(cluster, normaliser, limit, own, back, table, out):
    columns = out.shape[3]
    mask = own[...]
    rows = back[0]
    operands = [mask * rows[x : x + 1, :] for x in range(8)]
    result = lax.dot_general(
        jnp.concatenate(operands, axis=0).astype(jnp.bfloat16),
        table[0],
        (((1,), (1,)), ((), ())),
        preferred_element_type=jnp.float32,
    )
    first = lax.broadcasted_iota(jnp.int32, (cluster, columns), 1) < limit[...]
    for x in range(4):
        one = result[2 * x * cluster : (2 * x + 1) * cluster, :columns]
        two = result[(2 * x + 1) * cluster : (2 * x + 2) * cluster, :columns]
        out[x // 2, x % 2] = (jnp.where(first, one, two) * normaliser).astype(jnp.bfloat16)


def cluster_of(pairs):
    return 16 if pairs % 16 == 0 else pairs


def own_mask(cluster, rows):
    lane = jnp.arange(cluster * rows, dtype=jnp.int32)[None, :] // rows
    return (lane == jnp.arange(cluster, dtype=jnp.int32)[:, None]).astype(jnp.float32)


def legendre(spec, pair_ids, cos_lat, log_sin, truncation):
    pairs = pair_ids.shape[0]
    rows = cos_lat.shape[0]
    groups = pairs * rows // LANES
    group_pad = -(-groups // 8) * 8
    blocks = -(-pairs // 80)
    part = pairs // blocks
    cluster = cluster_of(pairs)
    clusters = pairs // cluster
    wide = cluster * rows
    chunks = -(-(truncation + 2) // CHUNK)
    diag1, diag2 = diagonals(pair_ids, log_sin, truncation)

    def lay(x):
        x = jnp.broadcast_to(x, (pairs, rows)).reshape(groups, LANES)
        return jnp.pad(x, ((0, group_pad - groups), (0, 0)))

    ids = jnp.tile(pair_ids.reshape(blocks, part), (1, 3))
    ids = jnp.pad(ids, ((0, 0), (0, 256 - 3 * part)))
    source = jnp.arange(256, dtype=jnp.int32)[:, None]
    target = jnp.arange(part * rows, dtype=jnp.int32)[None, :] // rows
    spread = ((source % part == target) & (source < 3 * part)).astype(jnp.bfloat16)
    whole = pl.BlockSpec(memory_space=pltpu.VMEM)
    tall = pltpu.VMEM((CHUNK * group_pad, LANES), jnp.float32)
    state = pltpu.VMEM((group_pad, LANES), jnp.float32)
    limit = truncation + 1 - pair_ids[:, None]

    def kernel(*refs):
        legendre_kernel(truncation, groups, group_pad, blocks, part, cluster, *refs)

    return pl.pallas_call(
        kernel,
        grid=(chunks,),
        in_specs=[whole] * 9,
        out_specs=(pl.BlockSpec((clusters, CHUNK, wide), lambda i: (0, i, 0)), whole),
        out_shape=(
            jax.ShapeDtypeStruct((clusters, chunks * CHUNK, wide), jnp.bfloat16),
            jax.ShapeDtypeStruct((clusters, 8, wide), jnp.float32),
        ),
        scratch_shapes=[
            tall, tall, tall, state, state,
            pltpu.VMEM((clusters, chunks * CHUNK, wide), jnp.bfloat16),
        ],
        compiler_params=pltpu.CompilerParams(vmem_limit_bytes=26 * 2**20),
        name="legendre",
    )(
        ids, spread, lay(cos_lat[None, :]), lay(diag1), lay(diag2), lay(limit), limit,
        own_mask(cluster, rows), spec,
    )


def adjoint(back, table, pair_ids, rows, columns, normaliser):
    pairs = pair_ids.shape[0]
    cluster = cluster_of(pairs)
    wide = cluster * rows
    limit = columns - 1 - pair_ids[:, None]

    def kernel(*refs):
        adjoint_kernel(cluster, normaliser, *refs)

    return pl.pallas_call(
        kernel,
        grid=(pairs // cluster,),
        in_specs=[
            pl.BlockSpec((cluster, 1), lambda i: (i, 0)),
            pl.BlockSpec((cluster, wide), lambda i: (0, 0)),
            pl.BlockSpec((1, 8, wide), lambda i: (i, 0, 0)),
            pl.BlockSpec((1, table.shape[1], wide), lambda i: (i, 0, 0)),
        ],
        out_specs=pl.BlockSpec((2, 2, cluster, columns), lambda i: (0, 0, i, 0)),
        out_shape=jax.ShapeDtypeStruct((2, 2, pairs, columns), jnp.bfloat16),
        compiler_params=pltpu.CompilerParams(vmem_limit_bytes=10 * 2**20),
        name="adjoint",
    )(limit, own_mask(cluster, rows), back, table)


def slot_table(row_map, owners, row_cap):
    onehot = (row_map[:, None] == jnp.arange(owners, dtype=jnp.int32)[None, :]).astype(jnp.int32)
    ranking = jnp.sum((jnp.cumsum(onehot, axis=0) - onehot) * onehot, axis=1)
    slot_of_row = row_map * row_cap + ranking
    return slot_of_row[None, :] == jnp.arange(owners * row_cap, dtype=jnp.int32)[:, None]


def angle_tables(lengths, orders, points):
    safe_len = jnp.maximum(lengths, 1)[:, None, None]
    step_angle = 2.0 * math.pi / safe_len.astype(jnp.float32)
    angles = (points[None, :, None] * orders[None, None, :] % safe_len).astype(
        jnp.float32
    ) * step_angle
    return jnp.cos(angles), jnp.sin(angles)


TILES = 7


def fourier_kernel(
    blocks, length, stacked, weight, low_c, low_s, row_c, row_s, col_c, col_s, twl_c, twl_s,
    twh_c, twh_s, grid, back, total,
):
    count = length[pl.program_id(0)]
    fields = weight.shape[1]
    half = fields // 2
    chunks = row_c.shape[1]
    total[...] = jnp.zeros_like(total)

    @pl.loop(0, chunks)
    def _(it):
        base_c, base_s = low_c[0], low_s[0]
        synth, analysis = [], []
        for j in range(TILES):
            far_c, far_s = col_c[0, it, :, j : j + 1], col_s[0, it, :, j : j + 1]
            cosine = (base_c * far_c - base_s * far_s).astype(jnp.bfloat16)
            sine = (base_s * far_c + base_c * far_s).astype(jnp.bfloat16)
            synth.append((cosine, sine))
            far_c, far_s = row_c[0, it, j : j + 1, :], row_s[0, it, j : j + 1, :]
            cosine = (base_c * far_c - base_s * far_s).astype(jnp.bfloat16)
            sine = (base_s * far_c + base_c * far_s).astype(jnp.bfloat16)
            analysis.append((cosine, sine))
        source = stacked[0]
        added = total[...]
        for j in range(TILES):
            cosine, sine = synth[j]
            table = jnp.concatenate(
                [
                    jnp.concatenate([cosine, sine], axis=1),
                    jnp.concatenate([-sine, cosine], axis=1),
                ],
                axis=0,
            )
            both = jnp.dot(source, table, preferred_element_type=jnp.float32)
            far_c, far_s = twh_c[0, it, :, j : j + 1], twh_s[0, it, :, j : j + 1]
            near_c, near_s = twl_c[0], twl_s[0]
            turn_c = near_c * far_c - near_s * far_s
            turn_s = near_s * far_c + near_c * far_s
            values = jnp.zeros((fields, LANES), jnp.float32)
            for q in range(blocks):
                rows = slice(q * fields, (q + 1) * fields)
                values += turn_c[q : q + 1] * both[rows, :LANES]
                values -= turn_s[q : q + 1] * both[rows, LANES:]
            first = (it * TILES + j) * LANES
            point = lax.broadcasted_iota(jnp.int32, (fields, LANES), 1) + first
            values = jnp.where(point < count, values, 0.0)
            lanes = pl.ds(pl.multiple_of(first, LANES), LANES)
            grid[0, 0, :, lanes] = values[:half]
            grid[0, 1, :, lanes] = values[half:]
            weighted = values * weight[0, :, lanes]
            turned = [
                jnp.concatenate(
                    [weighted * turn_c[q : q + 1], -(weighted * turn_s[q : q + 1])], axis=1
                )
                for q in range(blocks)
            ]
            turned = jnp.concatenate(turned, axis=0).astype(jnp.bfloat16)
            cosine, sine = analysis[j]
            table = jnp.concatenate(
                [
                    jnp.concatenate([cosine, -sine], axis=1),
                    jnp.concatenate([sine, cosine], axis=1),
                ],
                axis=0,
            )
            added += jnp.dot(turned, table, preferred_element_type=jnp.float32)
        total[...] = added

    back[0] = total[...].astype(jnp.bfloat16)


def fourier_both_ways(stacked, weight, lengths, blocks):
    slots, rows, _ = stacked.shape
    fields = rows // blocks
    row_points = weight.shape[2]
    chunks = -(-row_points // (TILES * LANES))
    points = chunks * TILES * LANES
    low = jnp.arange(LANES, dtype=jnp.int32)
    high = jnp.arange(chunks * TILES, dtype=jnp.int32) * LANES
    inner = jnp.arange(SUBW, dtype=jnp.int32)
    outer = jnp.arange(blocks, dtype=jnp.int32) * SUBW

    def cut(x, y):
        return x.reshape(slots, chunks, TILES, y)

    def turn(x, y):
        return jnp.swapaxes(cut(x, y), 2, 3)

    low_c, low_s = angle_tables(lengths, inner, low)
    high_c, high_s = angle_tables(lengths, inner, high)
    twl_c, twl_s = angle_tables(lengths, low, outer)
    twh_c, twh_s = angle_tables(lengths, outer, high)
    weight = jnp.tile(weight.astype(jnp.float32), (1, 2, 1))
    weight = jnp.pad(weight, ((0, 0), (0, 0), (0, points - row_points)))
    operands = [
        stacked, weight, low_c, low_s, cut(high_c, SUBW), cut(high_s, SUBW),
        turn(high_c, SUBW), turn(high_s, SUBW), twl_c, twl_s, turn(twh_c, blocks),
        turn(twh_s, blocks),
    ]

    def slot_block(shape):
        return pl.BlockSpec((1,) + shape[1:], lambda i: (i,) + (0,) * (len(shape) - 1))

    grid_shape = (slots, 2, fields // 2, points)

    def kernel(*refs):
        fourier_kernel(blocks, *refs)

    return pl.pallas_call(
        kernel,
        grid=(slots,),
        in_specs=[pl.BlockSpec(memory_space=pltpu.SMEM)] + [slot_block(x.shape) for x in operands],
        out_specs=(slot_block(grid_shape), slot_block(stacked.shape)),
        out_shape=(
            jax.ShapeDtypeStruct(grid_shape, jnp.float32),
            jax.ShapeDtypeStruct(stacked.shape, jnp.bfloat16),
        ),
        scratch_shapes=[pltpu.VMEM((rows, 2 * SUBW), jnp.float32)],
        compiler_params=pltpu.CompilerParams(vmem_limit_bytes=24 * 2**20),
        name="fourier",
    )(lengths, *operands)


def body(spec_in, observation_weight, latitude_row_length, wave_map, row_map):
    bands = lax.axis_size("band")
    levels = lax.axis_size("lev")
    owners = bands * levels
    owner_index = lax.axis_index("band") * levels + lax.axis_index("lev")
    columns = spec_in.shape[4]
    truncation = columns - 2
    waves_all = truncation + 1
    blocks = waves_all // SUBW
    row_cap = observation_weight.shape[0]
    row_points = observation_weight.shape[2]
    rows = latitude_row_length.shape[0]
    pairs = spec_in.shape[3]
    cos_lat, log_sin = latitudes(latitude_row_length, (row_points - 16) // 4)
    pair_ids = lax.dynamic_slice_in_dim(wave_map, lax.axis_index("band") * pairs, pairs)
    functions, fourier = legendre(spec_in[:, :, 0], pair_ids, cos_lat, log_sin, truncation)
    clusters = functions.shape[0]
    cluster = pairs // clusters
    fourier = fourier.astype(jnp.bfloat16).reshape(clusters, 2, 2, 2, cluster, rows)
    fourier = jnp.transpose(fourier, (5, 1, 2, 0, 4, 3)).reshape(rows, -1)

    chosen = slot_table(row_map, owners, row_cap)
    picker = chosen.astype(jnp.bfloat16)
    outgoing = jnp.dot(picker, fourier, preferred_element_type=jnp.float32).astype(jnp.bfloat16)
    outgoing = outgoing.reshape(owners, row_cap * 4, 2 * pairs)
    arrived = lax.all_to_all(outgoing, ("band", "lev"), split_axis=0, concat_axis=0, tiled=True)
    arrived = arrived.reshape(bands, levels, row_cap, 2, 2, 2 * pairs)
    arrived = jnp.transpose(arrived, (2, 3, 1, 4, 0, 5)).reshape(-1, waves_all)
    doubled = jnp.repeat(wave_map, 2)
    odd = jnp.arange(waves_all, dtype=jnp.int32) % 2
    m_of_w = jnp.where(odd == 0, doubled, truncation - doubled)
    order = jnp.arange(waves_all, dtype=jnp.int32)
    gain = jnp.where(order == 0, 1.0, 2.0)
    permute = jnp.where(m_of_w[:, None] == order[None, :], gain[None, :], 0.0).astype(jnp.bfloat16)
    scaled = jnp.dot(arrived, permute, preferred_element_type=jnp.float32).astype(jnp.bfloat16)
    scaled = scaled.reshape(row_cap, 2, levels, 2, blocks, SUBW)
    stacked = jnp.transpose(scaled, (0, 4, 1, 2, 3, 5)).reshape(row_cap, -1, 2 * SUBW)

    slot_length = jnp.sum(jnp.where(chosen, latitude_row_length[None, :], 0), axis=1)
    lengths = lax.dynamic_slice_in_dim(slot_length, owner_index * row_cap, row_cap)
    grid, back = fourier_both_ways(stacked, observation_weight, lengths, blocks)
    grid_incr = grid[..., :row_points]
    back = back.reshape(row_cap, blocks, 2, levels, 2, SUBW)
    back = jnp.transpose(back, (0, 2, 3, 4, 1, 5))
    back = back.reshape(-1, waves_all)
    back = lax.dot_general(
        back, permute, (((1,), (1,)), ((), ())), preferred_element_type=jnp.float32
    ).astype(jnp.bfloat16)
    back = back.reshape(row_cap, 2, levels, 2, bands, 2 * pairs)
    returning = jnp.transpose(back, (4, 2, 0, 1, 3, 5)).reshape(owners, row_cap * 4, 2 * pairs)
    returned = lax.all_to_all(returning, ("band", "lev"), split_axis=0, concat_axis=0, tiled=True)
    by_row = jnp.dot(
        picker.T, returned.reshape(owners * row_cap, -1), preferred_element_type=jnp.float32
    ).astype(jnp.bfloat16)
    by_row = by_row.reshape(rows, 2, 2, clusters, cluster, 2)
    by_row = jnp.transpose(by_row, (3, 1, 2, 5, 4, 0)).reshape(clusters, 8, cluster * rows)
    normaliser = 1.0 / math.sqrt(rows * row_points)
    gradient = adjoint(
        by_row.astype(jnp.float32), functions, pair_ids, rows, columns, normaliser
    )
    return (grid_incr, gradient[:, :, None])


def solution(mesh):
    return jax.shard_map(
        body,
        mesh=mesh,
        in_specs=(
            P("member", None, "lev", "band", None),
            P(("band", "lev"), "member", None),
            P(),
            P(),
            P(),
        ),
        out_specs=(
            P(("band", "lev"), None, "member", None),
            P("member", None, "lev", "band", None),
        ),
        check_vma=False,
    )
```

```python
import math

import jax
import jax.numpy as jnp
from jax import lax
from jax.experimental import pallas as pl
from jax.experimental.pallas import tpu as pltpu
from jax.sharding import PartitionSpec as P

SUBW = 128
LANES = 128
CHUNK = 144


def latitudes(latitude_row_length, halves):
    cycle_no = ((latitude_row_length - 16) // 4).astype(jnp.float32)
    colat = math.pi * (cycle_no - 0.25) / (2.0 * halves + 0.5)
    north = (
        jnp.arange(latitude_row_length.shape[0], dtype=jnp.int32)
        < latitude_row_length.shape[0] // 2
    )
    return (jnp.where(north, jnp.cos(colat), -jnp.cos(colat)), jnp.log(jnp.sin(colat)))


def diagonals(pair_ids, log_sin, truncation):
    first_order = pair_ids[:, None]
    counter = jnp.arange(1, truncation + 1, dtype=jnp.int32)
    log_terms = jnp.log(1.0 - 0.5 / counter.astype(jnp.float32))

    def start(orders):
        partial_sum = jnp.sum(
            jnp.where(counter[None, :] <= orders, log_terms[None, :], 0.0), axis=1, keepdims=True
        )
        order_m = orders.astype(jnp.float32)
        log_start = 0.5 * (jnp.log(order_m + 0.5) + partial_sum)
        return jnp.exp(log_start + order_m * log_sin[None, :])

    return (start(first_order), start(truncation - first_order))


def legendre_kernel(
    truncation, groups, group_pad, blocks, part, cluster, ids, spread, mu, diag1, diag2, bound,
    limit, own, spec, out, fourier, slopes, laggeds, values, newer, older, kept, epsilon, sems,
):
    step = pl.program_id(0)
    half = groups // blocks
    wide_lanes = kept.shape[2]
    tiles = wide_lanes // LANES

    @pl.when(step == 0)
    def _():
        newer[...] = jnp.zeros_like(newer)
        older[...] = diag1[...]
        epsilon[...] = jnp.zeros_like(epsilon)

    column = lax.broadcasted_iota(jnp.int32, (CHUNK, 256), 0) + step * CHUNK
    lane = lax.broadcasted_iota(jnp.int32, (CHUNK, 256), 1)

    def split(x):
        high = x.astype(jnp.bfloat16).astype(jnp.float32)
        rest = x - high
        middle = rest.astype(jnp.bfloat16).astype(jnp.float32)
        low = rest - middle
        piece = jnp.where(lane < part, high, jnp.where(lane < 2 * part, middle, low))
        return piece.astype(jnp.bfloat16)

    for b in range(blocks):
        first_order = ids[b : b + 1, :]
        boundary = truncation + 1 - first_order
        first_side = column < boundary
        order_m = jnp.where(first_side, first_order, truncation - first_order).astype(jnp.float32)
        degree = jnp.where(first_side, first_order + column, column - 1).astype(jnp.float32)
        restart_first = column == 0
        restart = restart_first | (column == boundary)

        upper = jnp.maximum(degree * degree - order_m * order_m, 0.0)
        lower = jnp.maximum(4.0 * degree * degree - 1.0, 1.0)
        ratio = upper / lower
        inverse = lax.rsqrt(jnp.where(restart, 1.0, ratio))
        slope = jnp.where(restart, 0.0, inverse)
        epsilon[b, 8:, :] = ratio * inverse
        before = epsilon[b, 7 : 7 + CHUNK, :]
        epsilon[b, 0:8, :] = epsilon[b, CHUNK : CHUNK + 8, :]
        lagged = jnp.where(restart_first, 1.0, -(before * slope))
        for table, compact in ((slopes, slope), (laggeds, lagged)):
            wide = jnp.dot(split(compact), spread[...], preferred_element_type=jnp.float32)
            for g in range(half):
                table[pl.ds(b * half + g, CHUNK, stride=group_pad), :] = wide[
                    :, g * LANES : (g + 1) * LANES
                ]

    mu_v = mu[...]
    diag2_v = diag2[...]
    bound_v = bound[...]

    def advance(i, carry):
        new, old = carry
        rows = pl.ds(pl.multiple_of(i * group_pad, 8), group_pad)
        lag = jnp.where(bound_v == step * CHUNK + i, diag2_v, laggeds[rows, :] * old)
        value = slopes[rows, :] * mu_v * new + lag
        values[rows, :] = value
        return (value, new)

    new, old = lax.fori_loop(0, CHUNK, advance, (newer[...], older[...]), unroll=16)
    newer[...] = new
    older[...] = old
    here = pl.ds(pl.multiple_of(step * CHUNK, CHUNK), CHUNK)
    for g in range(groups):
        piece = values[pl.ds(g, CHUNK, stride=group_pad), :].astype(jnp.bfloat16)
        lanes = pl.ds((g % tiles) * LANES, LANES)
        kept[g // tiles, here, lanes] = piece

    def outward(i):
        rows = pl.ds(pl.multiple_of(i * CHUNK, CHUNK), CHUNK)
        return pltpu.make_async_copy(kept.at[:, rows, :], out.at[:, rows, :], sems.at[i])

    outward(step).start()

    @pl.when(step == pl.num_programs(0) - 1)
    def _():
        columns = spec.shape[3]
        point = lax.broadcasted_iota(jnp.int32, (cluster, columns), 1)
        for k in range(groups // tiles):
            pairs = pl.ds(k * cluster, cluster)
            first = jnp.where(point < limit[pairs, :], 1.0, 0.0).astype(jnp.bfloat16)
            table = kept[k, :columns, :]
            operands = []
            for f in range(2):
                for i in range(2):
                    x = spec[f, i, pairs, :]
                    y = x * first
                    operands += [y, x - y]
            product = jnp.dot(
                jnp.concatenate(operands, axis=0), table, preferred_element_type=jnp.float32
            )
            product = product.reshape(8, cluster, wide_lanes) * own[...][None]
            fourier[k] = jnp.sum(product, axis=1)
        for i in range(kept.shape[1] // CHUNK):
            outward(i).wait()


def adjoint_kernel(cluster, normaliser, limit, own, back, table, out):
    columns = out.shape[3]
    mask = own[...]
    rows = back[0]
    operands = [mask * rows[x : x + 1, :] for x in range(8)]
    result = lax.dot_general(
        jnp.concatenate(operands, axis=0).astype(jnp.bfloat16),
        table[0],
        (((1,), (1,)), ((), ())),
        preferred_element_type=jnp.float32,
    )
    first = lax.broadcasted_iota(jnp.int32, (cluster, columns), 1) < limit[...]
    for x in range(4):
        one = result[2 * x * cluster : (2 * x + 1) * cluster, :columns]
        two = result[(2 * x + 1) * cluster : (2 * x + 2) * cluster, :columns]
        out[x // 2, x % 2] = (jnp.where(first, one, two) * normaliser).astype(jnp.bfloat16)


def cluster_of(pairs):
    return 16 if pairs % 16 == 0 else pairs


def own_mask(cluster, rows):
    lane = jnp.arange(cluster * rows, dtype=jnp.int32)[None, :] // rows
    return (lane == jnp.arange(cluster, dtype=jnp.int32)[:, None]).astype(jnp.float32)


def legendre(spec, pair_ids, cos_lat, log_sin, truncation):
    pairs = pair_ids.shape[0]
    rows = cos_lat.shape[0]
    groups = pairs * rows // LANES
    group_pad = -(-groups // 8) * 8
    blocks = -(-pairs // 80)
    part = pairs // blocks
    cluster = cluster_of(pairs)
    clusters = pairs // cluster
    wide = cluster * rows
    chunks = -(-(truncation + 2) // CHUNK)
    diag1, diag2 = diagonals(pair_ids, log_sin, truncation)

    def lay(x):
        x = jnp.broadcast_to(x, (pairs, rows)).reshape(groups, LANES)
        return jnp.pad(x, ((0, group_pad - groups), (0, 0)))

    ids = jnp.tile(pair_ids.reshape(blocks, part), (1, 3))
    ids = jnp.pad(ids, ((0, 0), (0, 256 - 3 * part)))
    source = jnp.arange(256, dtype=jnp.int32)[:, None]
    target = jnp.arange(part * rows, dtype=jnp.int32)[None, :] // rows
    spread = ((source % part == target) & (source < 3 * part)).astype(jnp.bfloat16)
    whole = pl.BlockSpec(memory_space=pltpu.VMEM)
    tall = pltpu.VMEM((CHUNK * group_pad, LANES), jnp.float32)
    state = pltpu.VMEM((group_pad, LANES), jnp.float32)
    limit = truncation + 1 - pair_ids[:, None]

    def kernel(*refs):
        legendre_kernel(truncation, groups, group_pad, blocks, part, cluster, *refs)

    return pl.pallas_call(
        kernel,
        grid=(chunks,),
        in_specs=[whole] * 9,
        out_specs=(pl.BlockSpec(memory_space=pltpu.HBM), whole),
        out_shape=(
            jax.ShapeDtypeStruct((clusters, chunks * CHUNK, wide), jnp.bfloat16),
            jax.ShapeDtypeStruct((clusters, 8, wide), jnp.float32),
        ),
        scratch_shapes=[
            tall, tall, tall, state, state,
            pltpu.VMEM((clusters, chunks * CHUNK, wide), jnp.bfloat16),
            pltpu.VMEM((blocks, CHUNK + 8, 256), jnp.float32),
            pltpu.SemaphoreType.DMA((chunks,)),
        ],
        compiler_params=pltpu.CompilerParams(vmem_limit_bytes=26 * 2**20),
        name="legendre",
    )(
        ids, spread, lay(cos_lat[None, :]), lay(diag1), lay(diag2), lay(limit), limit,
        own_mask(cluster, rows), spec,
    )


def adjoint(back, table, pair_ids, rows, columns, normaliser):
    pairs = pair_ids.shape[0]
    cluster = cluster_of(pairs)
    wide = cluster * rows
    limit = columns - 1 - pair_ids[:, None]

    def kernel(*refs):
        adjoint_kernel(cluster, normaliser, *refs)

    return pl.pallas_call(
        kernel,
        grid=(pairs // cluster,),
        in_specs=[
            pl.BlockSpec((cluster, 1), lambda i: (i, 0)),
            pl.BlockSpec((cluster, wide), lambda i: (0, 0)),
            pl.BlockSpec((1, 8, wide), lambda i: (i, 0, 0)),
            pl.BlockSpec((1, table.shape[1], wide), lambda i: (i, 0, 0)),
        ],
        out_specs=pl.BlockSpec((2, 2, cluster, columns), lambda i: (0, 0, i, 0)),
        out_shape=jax.ShapeDtypeStruct((2, 2, pairs, columns), jnp.bfloat16),
        compiler_params=pltpu.CompilerParams(vmem_limit_bytes=10 * 2**20),
        name="adjoint",
    )(limit, own_mask(cluster, rows), back, table)


def slot_table(row_map, owners, row_cap):
    onehot = (row_map[:, None] == jnp.arange(owners, dtype=jnp.int32)[None, :]).astype(jnp.int32)
    ranking = jnp.sum((jnp.cumsum(onehot, axis=0) - onehot) * onehot, axis=1)
    slot_of_row = row_map * row_cap + ranking
    return slot_of_row[None, :] == jnp.arange(owners * row_cap, dtype=jnp.int32)[:, None]


TILES = 7


def fourier_kernel(
    blocks, length, stacked, weight, trig_c, trig_s, col_c, col_s, twh_c, twh_s, grid, back,
    total, low_c, low_s,
):
    count = length[pl.program_id(0)]
    fields = weight.shape[1]
    half = fields // 2
    chunks = col_c.shape[1]
    total[...] = jnp.zeros_like(total)
    unit_c, unit_s = trig_c[0, 0:8, :], trig_s[0, 0:8, :]
    for a in range(LANES // 8):
        far_c, far_s = trig_c[0, 8 + a : 9 + a, :], trig_s[0, 8 + a : 9 + a, :]
        low_c[8 * a : 8 * a + 8, :] = unit_c * far_c - unit_s * far_s
        low_s[8 * a : 8 * a + 8, :] = unit_s * far_c + unit_c * far_s
    turn_row = trig_c.shape[1] - 16

    @pl.loop(0, chunks)
    def _(it):
        base_c, base_s = low_c[...], low_s[...]
        synth, analysis = [], []
        for j in range(TILES):
            far_c, far_s = col_c[0, it, :, j : j + 1], col_s[0, it, :, j : j + 1]
            cosine = (base_c * far_c - base_s * far_s).astype(jnp.bfloat16)
            sine = (base_s * far_c + base_c * far_s).astype(jnp.bfloat16)
            synth.append((cosine, sine))
            row = pl.ds(24 + it * TILES + j, 1)
            far_c, far_s = trig_c[0, row, :], trig_s[0, row, :]
            cosine = (base_c * far_c - base_s * far_s).astype(jnp.bfloat16)
            sine = (base_s * far_c + base_c * far_s).astype(jnp.bfloat16)
            analysis.append((cosine, sine))
        source = stacked[0]
        added = total[...]
        for j in range(TILES):
            cosine, sine = synth[j]
            table = jnp.concatenate(
                [
                    jnp.concatenate([cosine, sine], axis=1),
                    jnp.concatenate([-sine, cosine], axis=1),
                ],
                axis=0,
            )
            both = jnp.dot(source, table, preferred_element_type=jnp.float32)
            far_c, far_s = twh_c[0, it, :, j : j + 1], twh_s[0, it, :, j : j + 1]
            rows = slice(turn_row, turn_row + blocks)
            near_c, near_s = trig_c[0, rows, :], trig_s[0, rows, :]
            turn_c = near_c * far_c - near_s * far_s
            turn_s = near_s * far_c + near_c * far_s
            values = jnp.zeros((fields, LANES), jnp.float32)
            for q in range(blocks):
                rows = slice(q * fields, (q + 1) * fields)
                values += turn_c[q : q + 1] * both[rows, :LANES]
                values -= turn_s[q : q + 1] * both[rows, LANES:]
            first = (it * TILES + j) * LANES
            point = lax.broadcasted_iota(jnp.int32, (fields, LANES), 1) + first
            values = jnp.where(point < count, values, 0.0)
            lanes = pl.ds(pl.multiple_of(first, LANES), LANES)
            grid[0, 0, :, lanes] = values[:half]
            grid[0, 1, :, lanes] = values[half:]
            weighted = values * weight[0, :, lanes]
            turned = [
                jnp.concatenate(
                    [weighted * turn_c[q : q + 1], -(weighted * turn_s[q : q + 1])], axis=1
                )
                for q in range(blocks)
            ]
            turned = jnp.concatenate(turned, axis=0).astype(jnp.bfloat16)
            cosine, sine = analysis[j]
            table = jnp.concatenate(
                [
                    jnp.concatenate([cosine, -sine], axis=1),
                    jnp.concatenate([sine, cosine], axis=1),
                ],
                axis=0,
            )
            added += jnp.dot(turned, table, preferred_element_type=jnp.float32)
        total[...] = added

    back[0] = total[...].astype(jnp.bfloat16)


def fourier_both_ways(stacked, weight, lengths, blocks):
    slots, rows, _ = stacked.shape
    fields = rows // blocks
    row_points = weight.shape[2]
    chunks = -(-row_points // (TILES * LANES))
    points = chunks * TILES * LANES
    tiles = chunks * TILES
    lane = jnp.arange(LANES, dtype=jnp.int32)
    outer = jnp.arange(blocks, dtype=jnp.int32) * SUBW
    outer = jnp.pad(outer, (0, 16 - blocks))
    high = jnp.pad(lane[:tiles] * LANES, (0, -tiles % 8))
    factors = jnp.concatenate([lane[:8], lane[: LANES // 8] * 8, high, outer])
    products = factors[:, None] * lane[None, :]
    products = jnp.concatenate([products, outer[:, None] * (lane * LANES)[None, :]])
    safe_len = jnp.maximum(lengths, 1)[:, None, None]
    angles = (products[None] % safe_len).astype(jnp.float32)
    angles = angles * (2.0 * math.pi / safe_len.astype(jnp.float32))
    turn_row = 24 + high.shape[0]

    def arrange(x):
        col = x[:, 24 : 24 + tiles].reshape(slots, chunks, TILES, LANES)
        far = x[:, turn_row + 16 : turn_row + 16 + blocks, :tiles]
        far = far.reshape(slots, blocks, chunks, TILES)
        return x[:, : turn_row + 16], jnp.swapaxes(col, 2, 3), jnp.swapaxes(far, 1, 2)

    trig_c, col_c, twh_c = arrange(jnp.cos(angles))
    trig_s, col_s, twh_s = arrange(jnp.sin(angles))
    weight = jnp.tile(weight.astype(jnp.float32), (1, 2, 1))
    weight = jnp.pad(weight, ((0, 0), (0, 0), (0, points - row_points)))
    operands = [
        stacked, weight, trig_c, trig_s, col_c, col_s, twh_c, twh_s,
    ]

    def slot_block(shape):
        return pl.BlockSpec((1,) + shape[1:], lambda i: (i,) + (0,) * (len(shape) - 1))

    grid_shape = (slots, 2, fields // 2, points)

    def kernel(*refs):
        fourier_kernel(blocks, *refs)

    return pl.pallas_call(
        kernel,
        grid=(slots,),
        in_specs=[pl.BlockSpec(memory_space=pltpu.SMEM)] + [slot_block(x.shape) for x in operands],
        out_specs=(slot_block(grid_shape), slot_block(stacked.shape)),
        out_shape=(
            jax.ShapeDtypeStruct(grid_shape, jnp.float32),
            jax.ShapeDtypeStruct(stacked.shape, jnp.bfloat16),
        ),
        scratch_shapes=[
            pltpu.VMEM((rows, 2 * SUBW), jnp.float32),
            pltpu.VMEM((LANES, SUBW), jnp.float32),
            pltpu.VMEM((LANES, SUBW), jnp.float32),
        ],
        compiler_params=pltpu.CompilerParams(vmem_limit_bytes=24 * 2**20),
        name="fourier",
    )(lengths, *operands)


def body(spec_in, observation_weight, latitude_row_length, wave_map, row_map):
    bands = lax.axis_size("band")
    levels = lax.axis_size("lev")
    owners = bands * levels
    owner_index = lax.axis_index("band") * levels + lax.axis_index("lev")
    columns = spec_in.shape[4]
    truncation = columns - 2
    waves_all = truncation + 1
    blocks = waves_all // SUBW
    row_cap = observation_weight.shape[0]
    row_points = observation_weight.shape[2]
    rows = latitude_row_length.shape[0]
    pairs = spec_in.shape[3]
    cos_lat, log_sin = latitudes(latitude_row_length, (row_points - 16) // 4)
    pair_ids = lax.dynamic_slice_in_dim(wave_map, lax.axis_index("band") * pairs, pairs)
    functions, fourier = legendre(spec_in[:, :, 0], pair_ids, cos_lat, log_sin, truncation)
    clusters = functions.shape[0]
    cluster = pairs // clusters
    fourier = fourier.astype(jnp.bfloat16).reshape(clusters, 2, 2, 2, cluster, rows)
    fourier = jnp.transpose(fourier, (5, 1, 2, 0, 4, 3)).reshape(rows, -1)

    chosen = slot_table(row_map, owners, row_cap)
    picker = chosen.astype(jnp.bfloat16)
    outgoing = jnp.dot(picker, fourier, preferred_element_type=jnp.float32).astype(jnp.bfloat16)
    outgoing = outgoing.reshape(owners, row_cap * 4, 2 * pairs)
    arrived = lax.all_to_all(outgoing, ("band", "lev"), split_axis=0, concat_axis=0, tiled=True)
    arrived = arrived.reshape(bands, levels, row_cap, 2, 2, 2 * pairs)
    arrived = jnp.transpose(arrived, (2, 3, 1, 4, 0, 5)).reshape(-1, waves_all)
    doubled = jnp.repeat(wave_map, 2)
    odd = jnp.arange(waves_all, dtype=jnp.int32) % 2
    m_of_w = jnp.where(odd == 0, doubled, truncation - doubled)
    order = jnp.arange(waves_all, dtype=jnp.int32)
    gain = jnp.where(order == 0, 1.0, 2.0)
    permute = jnp.where(m_of_w[:, None] == order[None, :], gain[None, :], 0.0).astype(jnp.bfloat16)
    scaled = jnp.dot(arrived, permute, preferred_element_type=jnp.float32).astype(jnp.bfloat16)
    scaled = scaled.reshape(row_cap, 2, levels, 2, blocks, SUBW)
    stacked = jnp.transpose(scaled, (0, 4, 1, 2, 3, 5)).reshape(row_cap, -1, 2 * SUBW)

    slot_length = jnp.sum(jnp.where(chosen, latitude_row_length[None, :], 0), axis=1)
    lengths = lax.dynamic_slice_in_dim(slot_length, owner_index * row_cap, row_cap)
    grid, back = fourier_both_ways(stacked, observation_weight, lengths, blocks)
    grid_incr = grid[..., :row_points]
    back = back.reshape(row_cap, blocks, 2, levels, 2, SUBW)
    back = jnp.transpose(back, (0, 2, 3, 4, 1, 5))
    back = back.reshape(-1, waves_all)
    back = lax.dot_general(
        back, permute, (((1,), (1,)), ((), ())), preferred_element_type=jnp.float32
    ).astype(jnp.bfloat16)
    back = back.reshape(row_cap, 2, levels, 2, bands, 2 * pairs)
    returning = jnp.transpose(back, (4, 2, 0, 1, 3, 5)).reshape(owners, row_cap * 4, 2 * pairs)
    returned = lax.all_to_all(returning, ("band", "lev"), split_axis=0, concat_axis=0, tiled=True)
    by_row = jnp.dot(
        picker.T, returned.reshape(owners * row_cap, -1), preferred_element_type=jnp.float32
    ).astype(jnp.bfloat16)
    by_row = by_row.reshape(rows, 2, 2, clusters, cluster, 2)
    by_row = jnp.transpose(by_row, (3, 1, 2, 5, 4, 0)).reshape(clusters, 8, cluster * rows)
    normaliser = 1.0 / math.sqrt(rows * row_points)
    gradient = adjoint(
        by_row.astype(jnp.float32), functions, pair_ids, rows, columns, normaliser
    )
    return (grid_incr, gradient[:, :, None])


def solution(mesh):
    return jax.shard_map(
        body,
        mesh=mesh,
        in_specs=(
            P("member", None, "lev", "band", None),
            P(("band", "lev"), "member", None),
            P(),
            P(),
            P(),
        ),
        out_specs=(
            P(("band", "lev"), None, "member", None),
            P("member", None, "lev", "band", None),
        ),
        check_vma=False,
    )
```

```python
import math

import jax
import jax.numpy as jnp
from jax import lax
from jax.experimental import pallas as pl
from jax.experimental.pallas import tpu as pltpu
from jax.sharding import PartitionSpec as P

SUBW = 128
LANES = 128
CHUNK = 144


def latitudes(latitude_row_length, halves):
    cycle_no = ((latitude_row_length - 16) // 4).astype(jnp.float32)
    colat = math.pi * (cycle_no - 0.25) / (2.0 * halves + 0.5)
    north = (
        jnp.arange(latitude_row_length.shape[0], dtype=jnp.int32)
        < latitude_row_length.shape[0] // 2
    )
    return (jnp.where(north, jnp.cos(colat), -jnp.cos(colat)), jnp.log(jnp.sin(colat)))


def diagonals(pair_ids, log_sin, truncation):
    first_order = pair_ids[:, None]
    counter = jnp.arange(1, truncation + 1, dtype=jnp.int32)
    log_terms = jnp.log(1.0 - 0.5 / counter.astype(jnp.float32))

    def start(orders):
        partial_sum = jnp.sum(
            jnp.where(counter[None, :] <= orders, log_terms[None, :], 0.0), axis=1, keepdims=True
        )
        order_m = orders.astype(jnp.float32)
        log_start = 0.5 * (jnp.log(order_m + 0.5) + partial_sum)
        return jnp.exp(log_start + order_m * log_sin[None, :])

    return (start(first_order), start(truncation - first_order))


def legendre_kernel(
    truncation, groups, group_pad, blocks, part, cluster, ids, spread, mu, diag1, diag2, bound,
    limit, own, spec, out, fourier, slopes, laggeds, values, newer, older, kept, epsilon, sems,
):
    step = pl.program_id(0)
    half = groups // blocks
    wide_lanes = kept.shape[2]
    tiles = wide_lanes // LANES

    @pl.when(step == 0)
    def _():
        newer[...] = jnp.zeros_like(newer)
        older[...] = diag1[...]
        epsilon[...] = jnp.zeros_like(epsilon)

    column = lax.broadcasted_iota(jnp.int32, (CHUNK, 256), 0) + step * CHUNK
    lane = lax.broadcasted_iota(jnp.int32, (CHUNK, 256), 1)

    def split(x):
        high = x.astype(jnp.bfloat16).astype(jnp.float32)
        rest = x - high
        middle = rest.astype(jnp.bfloat16).astype(jnp.float32)
        low = rest - middle
        piece = jnp.where(lane < part, high, jnp.where(lane < 2 * part, middle, low))
        return piece.astype(jnp.bfloat16)

    for b in range(blocks):
        first_order = ids[b : b + 1, :]
        boundary = truncation + 1 - first_order
        first_side = column < boundary
        order_m = jnp.where(first_side, first_order, truncation - first_order).astype(jnp.float32)
        degree = jnp.where(first_side, first_order + column, column - 1).astype(jnp.float32)
        restart_first = column == 0
        restart = restart_first | (column == boundary)

        upper = jnp.maximum(degree * degree - order_m * order_m, 0.0)
        lower = jnp.maximum(4.0 * degree * degree - 1.0, 1.0)
        ratio = upper / lower
        inverse = lax.rsqrt(jnp.where(restart, 1.0, ratio))
        slope = jnp.where(restart, 0.0, inverse)
        epsilon[b, 8:, :] = ratio * inverse
        before = epsilon[b, 7 : 7 + CHUNK, :]
        epsilon[b, 0:8, :] = epsilon[b, CHUNK : CHUNK + 8, :]
        lagged = jnp.where(restart_first, 1.0, -(before * slope))
        for table, compact in ((slopes, slope), (laggeds, lagged)):
            wide = jnp.dot(split(compact), spread[...], preferred_element_type=jnp.float32)
            for g in range(half):
                table[pl.ds(b * half + g, CHUNK, stride=group_pad), :] = wide[
                    :, g * LANES : (g + 1) * LANES
                ]

    mu_v = mu[...]
    diag2_v = diag2[...]
    bound_v = bound[...]

    def advance(i, carry):
        new, old = carry
        rows = pl.ds(pl.multiple_of(i * group_pad, 8), group_pad)
        lag = jnp.where(bound_v == step * CHUNK + i, diag2_v, laggeds[rows, :] * old)
        value = slopes[rows, :] * mu_v * new + lag
        values[rows, :] = value
        return (value, new)

    new, old = lax.fori_loop(0, CHUNK, advance, (newer[...], older[...]), unroll=16)
    newer[...] = new
    older[...] = old
    here = pl.ds(pl.multiple_of(step * CHUNK, CHUNK), CHUNK)
    for g in range(groups):
        piece = values[pl.ds(g, CHUNK, stride=group_pad), :].astype(jnp.bfloat16)
        lanes = pl.ds((g % tiles) * LANES, LANES)
        kept[g // tiles, here, lanes] = piece

    def outward(i):
        rows = pl.ds(pl.multiple_of(i * CHUNK, CHUNK), CHUNK)
        return pltpu.make_async_copy(kept.at[:, rows, :], out.at[:, rows, :], sems.at[i])

    outward(step).start()

    @pl.when(step == pl.num_programs(0) - 1)
    def _():
        columns = spec.shape[3]
        point = lax.broadcasted_iota(jnp.int32, (cluster, columns), 1)
        for k in range(groups // tiles):
            pairs = pl.ds(k * cluster, cluster)
            first = jnp.where(point < limit[pairs, :], 1.0, 0.0).astype(jnp.bfloat16)
            table = kept[k, :columns, :]
            operands = []
            for f in range(2):
                for i in range(2):
                    x = spec[f, i, pairs, :]
                    y = x * first
                    operands += [y, x - y]
            product = jnp.dot(
                jnp.concatenate(operands, axis=0), table, preferred_element_type=jnp.float32
            )
            product = product.reshape(8, cluster, wide_lanes) * own[...][None]
            fourier[k] = jnp.sum(product, axis=1)
        for i in range(kept.shape[1] // CHUNK):
            outward(i).wait()


def adjoint_kernel(cluster, normaliser, limit, own, back, table, out):
    columns = out.shape[3]
    mask = own[...]
    rows = back[0]
    operands = [mask * rows[x : x + 1, :] for x in range(8)]
    result = lax.dot_general(
        jnp.concatenate(operands, axis=0).astype(jnp.bfloat16),
        table[0],
        (((1,), (1,)), ((), ())),
        preferred_element_type=jnp.float32,
    )
    first = lax.broadcasted_iota(jnp.int32, (cluster, columns), 1) < limit[...]
    for x in range(4):
        one = result[2 * x * cluster : (2 * x + 1) * cluster, :columns]
        two = result[(2 * x + 1) * cluster : (2 * x + 2) * cluster, :columns]
        out[x // 2, x % 2] = (jnp.where(first, one, two) * normaliser).astype(jnp.bfloat16)


def cluster_of(pairs):
    return 16 if pairs % 16 == 0 else pairs


def own_mask(cluster, rows):
    lane = jnp.arange(cluster * rows, dtype=jnp.int32)[None, :] // rows
    return (lane == jnp.arange(cluster, dtype=jnp.int32)[:, None]).astype(jnp.float32)


def legendre(spec, pair_ids, cos_lat, log_sin, truncation):
    pairs = pair_ids.shape[0]
    rows = cos_lat.shape[0]
    groups = pairs * rows // LANES
    group_pad = -(-groups // 8) * 8
    blocks = -(-pairs // 80)
    part = pairs // blocks
    cluster = cluster_of(pairs)
    clusters = pairs // cluster
    wide = cluster * rows
    chunks = -(-(truncation + 2) // CHUNK)
    diag1, diag2 = diagonals(pair_ids, log_sin, truncation)

    def lay(x):
        x = jnp.broadcast_to(x, (pairs, rows)).reshape(groups, LANES)
        return jnp.pad(x, ((0, group_pad - groups), (0, 0)))

    ids = jnp.tile(pair_ids.reshape(blocks, part), (1, 3))
    ids = jnp.pad(ids, ((0, 0), (0, 256 - 3 * part)))
    source = jnp.arange(256, dtype=jnp.int32)[:, None]
    target = jnp.arange(part * rows, dtype=jnp.int32)[None, :] // rows
    spread = ((source % part == target) & (source < 3 * part)).astype(jnp.bfloat16)
    whole = pl.BlockSpec(memory_space=pltpu.VMEM)
    tall = pltpu.VMEM((CHUNK * group_pad, LANES), jnp.float32)
    state = pltpu.VMEM((group_pad, LANES), jnp.float32)
    limit = truncation + 1 - pair_ids[:, None]

    def kernel(*refs):
        legendre_kernel(truncation, groups, group_pad, blocks, part, cluster, *refs)

    return pl.pallas_call(
        kernel,
        grid=(chunks,),
        in_specs=[whole] * 9,
        out_specs=(pl.BlockSpec(memory_space=pltpu.HBM), whole),
        out_shape=(
            jax.ShapeDtypeStruct((clusters, chunks * CHUNK, wide), jnp.bfloat16),
            jax.ShapeDtypeStruct((clusters, 8, wide), jnp.float32),
        ),
        scratch_shapes=[
            tall, tall, tall, state, state,
            pltpu.VMEM((clusters, chunks * CHUNK, wide), jnp.bfloat16),
            pltpu.VMEM((blocks, CHUNK + 8, 256), jnp.float32),
            pltpu.SemaphoreType.DMA((chunks,)),
        ],
        compiler_params=pltpu.CompilerParams(vmem_limit_bytes=54 * 2**20),
        name="legendre",
    )(
        ids, spread, lay(cos_lat[None, :]), lay(diag1), lay(diag2), lay(limit), limit,
        own_mask(cluster, rows), spec,
    )


def adjoint(back, table, pair_ids, rows, columns, normaliser):
    pairs = pair_ids.shape[0]
    cluster = cluster_of(pairs)
    wide = cluster * rows
    limit = columns - 1 - pair_ids[:, None]

    def kernel(*refs):
        adjoint_kernel(cluster, normaliser, *refs)

    return pl.pallas_call(
        kernel,
        grid=(pairs // cluster,),
        in_specs=[
            pl.BlockSpec((cluster, 1), lambda i: (i, 0)),
            pl.BlockSpec((cluster, wide), lambda i: (0, 0)),
            pl.BlockSpec((1, 8, wide), lambda i: (i, 0, 0)),
            pl.BlockSpec((1, table.shape[1], wide), lambda i: (i, 0, 0)),
        ],
        out_specs=pl.BlockSpec((2, 2, cluster, columns), lambda i: (0, 0, i, 0)),
        out_shape=jax.ShapeDtypeStruct((2, 2, pairs, columns), jnp.bfloat16),
        compiler_params=pltpu.CompilerParams(vmem_limit_bytes=10 * 2**20),
        name="adjoint",
    )(limit, own_mask(cluster, rows), back, table)


def slot_table(row_map, owners, row_cap):
    onehot = (row_map[:, None] == jnp.arange(owners, dtype=jnp.int32)[None, :]).astype(jnp.int32)
    ranking = jnp.sum((jnp.cumsum(onehot, axis=0) - onehot) * onehot, axis=1)
    slot_of_row = row_map * row_cap + ranking
    return slot_of_row[None, :] == jnp.arange(owners * row_cap, dtype=jnp.int32)[:, None]


TILES = 7


def fourier_kernel(
    blocks, length, stacked, weight, trig_c, trig_s, col_c, col_s, twh_c, twh_s, grid, back,
    total, low_c, low_s,
):
    count = length[pl.program_id(0)]
    fields = weight.shape[1]
    half = fields // 2
    chunks = col_c.shape[1]
    total[...] = jnp.zeros_like(total)
    unit_c, unit_s = trig_c[0, 0:8, :], trig_s[0, 0:8, :]
    for a in range(LANES // 8):
        far_c, far_s = trig_c[0, 8 + a : 9 + a, :], trig_s[0, 8 + a : 9 + a, :]
        low_c[8 * a : 8 * a + 8, :] = unit_c * far_c - unit_s * far_s
        low_s[8 * a : 8 * a + 8, :] = unit_s * far_c + unit_c * far_s
    turn_row = trig_c.shape[1] - 16

    @pl.loop(0, chunks)
    def _(it):
        base_c, base_s = low_c[...], low_s[...]
        synth, analysis = [], []
        for j in range(TILES):
            far_c, far_s = col_c[0, it, :, j : j + 1], col_s[0, it, :, j : j + 1]
            cosine = (base_c * far_c - base_s * far_s).astype(jnp.bfloat16)
            sine = (base_s * far_c + base_c * far_s).astype(jnp.bfloat16)
            synth.append((cosine, sine))
            row = pl.ds(24 + it * TILES + j, 1)
            far_c, far_s = trig_c[0, row, :], trig_s[0, row, :]
            cosine = (base_c * far_c - base_s * far_s).astype(jnp.bfloat16)
            sine = (base_s * far_c + base_c * far_s).astype(jnp.bfloat16)
            analysis.append((cosine, sine))
        source = stacked[0]
        added = total[...]
        for j in range(TILES):
            cosine, sine = synth[j]
            table = jnp.concatenate(
                [
                    jnp.concatenate([cosine, sine], axis=1),
                    jnp.concatenate([-sine, cosine], axis=1),
                ],
                axis=0,
            )
            both = jnp.dot(source, table, preferred_element_type=jnp.float32)
            far_c, far_s = twh_c[0, it, :, j : j + 1], twh_s[0, it, :, j : j + 1]
            rows = slice(turn_row, turn_row + blocks)
            near_c, near_s = trig_c[0, rows, :], trig_s[0, rows, :]
            turn_c = near_c * far_c - near_s * far_s
            turn_s = near_s * far_c + near_c * far_s
            values = jnp.zeros((fields, LANES), jnp.float32)
            for q in range(blocks):
                rows = slice(q * fields, (q + 1) * fields)
                values += turn_c[q : q + 1] * both[rows, :LANES]
                values -= turn_s[q : q + 1] * both[rows, LANES:]
            first = (it * TILES + j) * LANES
            point = lax.broadcasted_iota(jnp.int32, (fields, LANES), 1) + first
            values = jnp.where(point < count, values, 0.0)
            lanes = pl.ds(pl.multiple_of(first, LANES), LANES)
            grid[0, 0, :, lanes] = values[:half]
            grid[0, 1, :, lanes] = values[half:]
            weighted = values * weight[0, :, lanes]
            turned = [
                jnp.concatenate(
                    [weighted * turn_c[q : q + 1], -(weighted * turn_s[q : q + 1])], axis=1
                )
                for q in range(blocks)
            ]
            turned = jnp.concatenate(turned, axis=0).astype(jnp.bfloat16)
            cosine, sine = analysis[j]
            table = jnp.concatenate(
                [
                    jnp.concatenate([cosine, -sine], axis=1),
                    jnp.concatenate([sine, cosine], axis=1),
                ],
                axis=0,
            )
            added += jnp.dot(turned, table, preferred_element_type=jnp.float32)
        total[...] = added

    back[0] = total[...].astype(jnp.bfloat16)


def fourier_both_ways(stacked, weight, lengths, blocks):
    slots, rows, _ = stacked.shape
    fields = rows // blocks
    row_points = weight.shape[2]
    chunks = -(-row_points // (TILES * LANES))
    points = chunks * TILES * LANES
    tiles = chunks * TILES
    lane = jnp.arange(LANES, dtype=jnp.int32)
    outer = jnp.arange(blocks, dtype=jnp.int32) * SUBW
    outer = jnp.pad(outer, (0, 16 - blocks))
    high = jnp.pad(lane[:tiles] * LANES, (0, -tiles % 8))
    factors = jnp.concatenate([lane[:8], lane[: LANES // 8] * 8, high, outer])
    products = factors[:, None] * lane[None, :]
    products = jnp.concatenate([products, outer[:, None] * (lane * LANES)[None, :]])
    safe_len = jnp.maximum(lengths, 1)[:, None, None]
    angles = (products[None] % safe_len).astype(jnp.float32)
    angles = angles * (2.0 * math.pi / safe_len.astype(jnp.float32))
    turn_row = 24 + high.shape[0]

    def arrange(x):
        col = x[:, 24 : 24 + tiles].reshape(slots, chunks, TILES, LANES)
        far = x[:, turn_row + 16 : turn_row + 16 + blocks, :tiles]
        far = far.reshape(slots, blocks, chunks, TILES)
        return x[:, : turn_row + 16], jnp.swapaxes(col, 2, 3), jnp.swapaxes(far, 1, 2)

    trig_c, col_c, twh_c = arrange(jnp.cos(angles))
    trig_s, col_s, twh_s = arrange(jnp.sin(angles))
    weight = jnp.tile(weight.astype(jnp.float32), (1, 2, 1))
    weight = jnp.pad(weight, ((0, 0), (0, 0), (0, points - row_points)))
    operands = [
        stacked, weight, trig_c, trig_s, col_c, col_s, twh_c, twh_s,
    ]

    def slot_block(shape):
        return pl.BlockSpec((1,) + shape[1:], lambda i: (i,) + (0,) * (len(shape) - 1))

    grid_shape = (slots, 2, fields // 2, points)

    def kernel(*refs):
        fourier_kernel(blocks, *refs)

    return pl.pallas_call(
        kernel,
        grid=(slots,),
        in_specs=[pl.BlockSpec(memory_space=pltpu.SMEM)] + [slot_block(x.shape) for x in operands],
        out_specs=(slot_block(grid_shape), slot_block(stacked.shape)),
        out_shape=(
            jax.ShapeDtypeStruct(grid_shape, jnp.float32),
            jax.ShapeDtypeStruct(stacked.shape, jnp.bfloat16),
        ),
        scratch_shapes=[
            pltpu.VMEM((rows, 2 * SUBW), jnp.float32),
            pltpu.VMEM((LANES, SUBW), jnp.float32),
            pltpu.VMEM((LANES, SUBW), jnp.float32),
        ],
        compiler_params=pltpu.CompilerParams(vmem_limit_bytes=24 * 2**20),
        name="fourier",
    )(lengths, *operands)


def body(spec_in, observation_weight, latitude_row_length, wave_map, row_map):
    bands = lax.axis_size("band")
    levels = lax.axis_size("lev")
    owners = bands * levels
    owner_index = lax.axis_index("band") * levels + lax.axis_index("lev")
    columns = spec_in.shape[4]
    truncation = columns - 2
    waves_all = truncation + 1
    blocks = waves_all // SUBW
    row_cap = observation_weight.shape[0]
    row_points = observation_weight.shape[2]
    rows = latitude_row_length.shape[0]
    pairs = spec_in.shape[3]
    cos_lat, log_sin = latitudes(latitude_row_length, (row_points - 16) // 4)
    pair_ids = lax.dynamic_slice_in_dim(wave_map, lax.axis_index("band") * pairs, pairs)
    functions, fourier = legendre(spec_in[:, :, 0], pair_ids, cos_lat, log_sin, truncation)
    clusters = functions.shape[0]
    cluster = pairs // clusters
    fourier = fourier.astype(jnp.bfloat16).reshape(clusters, 2, 2, 2, cluster, rows)
    fourier = jnp.transpose(fourier, (5, 1, 2, 0, 4, 3)).reshape(rows, -1)

    chosen = slot_table(row_map, owners, row_cap)
    picker = chosen.astype(jnp.bfloat16)
    outgoing = jnp.dot(picker, fourier, preferred_element_type=jnp.float32).astype(jnp.bfloat16)
    outgoing = outgoing.reshape(owners, row_cap * 4, 2 * pairs)
    arrived = lax.all_to_all(outgoing, ("band", "lev"), split_axis=0, concat_axis=0, tiled=True)
    arrived = arrived.reshape(bands, levels, row_cap, 2, 2, 2 * pairs)
    arrived = jnp.transpose(arrived, (2, 3, 1, 4, 0, 5)).reshape(-1, waves_all)
    doubled = jnp.repeat(wave_map, 2)
    odd = jnp.arange(waves_all, dtype=jnp.int32) % 2
    m_of_w = jnp.where(odd == 0, doubled, truncation - doubled)
    order = jnp.arange(waves_all, dtype=jnp.int32)
    gain = jnp.where(order == 0, 1.0, 2.0)
    permute = jnp.where(m_of_w[:, None] == order[None, :], gain[None, :], 0.0).astype(jnp.bfloat16)
    scaled = jnp.dot(arrived, permute, preferred_element_type=jnp.float32).astype(jnp.bfloat16)
    scaled = scaled.reshape(row_cap, 2, levels, 2, blocks, SUBW)
    stacked = jnp.transpose(scaled, (0, 4, 1, 2, 3, 5)).reshape(row_cap, -1, 2 * SUBW)

    slot_length = jnp.sum(jnp.where(chosen, latitude_row_length[None, :], 0), axis=1)
    lengths = lax.dynamic_slice_in_dim(slot_length, owner_index * row_cap, row_cap)
    grid, back = fourier_both_ways(stacked, observation_weight, lengths, blocks)
    grid_incr = grid[..., :row_points]
    back = back.reshape(row_cap, blocks, 2, levels, 2, SUBW)
    back = jnp.transpose(back, (0, 2, 3, 4, 1, 5))
    back = back.reshape(-1, waves_all)
    back = lax.dot_general(
        back, permute, (((1,), (1,)), ((), ())), preferred_element_type=jnp.float32
    ).astype(jnp.bfloat16)
    back = back.reshape(row_cap, 2, levels, 2, bands, 2 * pairs)
    returning = jnp.transpose(back, (4, 2, 0, 1, 3, 5)).reshape(owners, row_cap * 4, 2 * pairs)
    returned = lax.all_to_all(returning, ("band", "lev"), split_axis=0, concat_axis=0, tiled=True)
    by_row = jnp.dot(
        picker.T, returned.reshape(owners * row_cap, -1), preferred_element_type=jnp.float32
    ).astype(jnp.bfloat16)
    by_row = by_row.reshape(rows, 2, 2, clusters, cluster, 2)
    by_row = jnp.transpose(by_row, (3, 1, 2, 5, 4, 0)).reshape(clusters, 8, cluster * rows)
    normaliser = 1.0 / math.sqrt(rows * row_points)
    gradient = adjoint(
        by_row.astype(jnp.float32), functions, pair_ids, rows, columns, normaliser
    )
    return (grid_incr, gradient[:, :, None])


def solution(mesh):
    return jax.shard_map(
        body,
        mesh=mesh,
        in_specs=(
            P("member", None, "lev", "band", None),
            P(("band", "lev"), "member", None),
            P(),
            P(),
            P(),
        ),
        out_specs=(
            P(("band", "lev"), None, "member", None),
            P("member", None, "lev", "band", None),
        ),
        check_vma=False,
    )
```
